128 devices in a mesh: tile: 32 (over x, z, core), chan: 4 (over y).
Axes of the slice: x: 4, y: 4, z: 4, core: 2. Of those that a mesh axis runs over, the one named last changes fastest.
Arguments:
- visibilities: float32 [4, 8192, 128], P('chan', 'tile'), may hold values from -6 to 6
- kernels: bfloat16 [4, 32, 2, 64, 128], P('chan'), may hold values from -0.75 to 0.75
- destination: int32 [4, 8192, 1], P('chan', 'tile'), may hold values from 0 to 31; in each aligned block of 256 rows (0 to 255, 256 to 511, ..., all dimensions but the last counted through in order) at most 24 rows name the same one
- cell: int32 [4, 8192], P('chan', 'tile'), may hold values from 0 to 511
- plane: int32 [4, 8192], P('chan', 'tile'), may hold values from 0 to 31
Outputs:
- image: float32 [1024, 1024], P('chan', 'tile')
The draws below stay inside these ranges and needn't reach their ends.
Inputs may be any that keep to these rules, and one draw needn't show every extreme that they name: `destination`: in the rows of one device (aligned blocks of 256 rows), no tile is named more than 24 times; some tile is named exactly 24 times in some devices' rows.
All inputs are finite; a program needn't handle non-finite values.
Results may differ from the reference program's by a relative error of at most 0.0059.
Values may be sent and summed in bfloat16 or wider, within the bound.
A program may use at most 320 MiB of HBM per device.

```python
import math
import jax
import jax.numpy as jnp
import numpy as np
from jax import lax

G = 8192
S = 64
K = 64
NW = 32
P_SIZE = 1024
BLK_DEV = 256
CAP = 24
NCG = 4
BASE = 8192
CELLS_T = 512
N_TILE = 32


def place_ends(drawn, key, least, largest):
    place = [jax.random.randint(jax.random.fold_in(key, axis), (), 0, length) for axis, length in enumerate(drawn.shape)]
    main_axis = drawn.shape.index(max(drawn.shape))
    beside = place[:main_axis] + [(place[main_axis] + 1) % drawn.shape[main_axis]] + place[main_axis + 1:]
    return drawn.at[tuple(place)].set(least).at[tuple(beside)].set(largest)


def shard_levels(own_key, shape, cuts, least, high):
    def one(axis_at, shards_of):
        heights = jax.random.uniform(jax.random.fold_in(jax.random.fold_in(own_key, 6), axis_at), (shards_of,), jnp.float32, least / len(cuts), high / len(cuts))
        return jnp.repeat(jnp.exp(heights), shape[axis_at] // shards_of).reshape((-1,) + (1,) * (len(shape) - axis_at - 1))

    factor_of = one(*cuts[0])
    for cut in cuts[1:]:
        factor_of = factor_of * one(*cut)
    return factor_of


def assign_block(own_key, own, number, rows, number_of, top, limit, skew):
    order = jax.random.permutation(own_key, number_of)
    heavy_load, common = shares(number_of, rows * top, limit, skew, True), shares(number_of, rows * top, limit, skew, False)
    places = jnp.arange(number_of)

    def named(sizes, rotation):
        used = int((sizes > 0).sum())
        fixed = max(1, used // 4)
        shifted = fixed + (places - fixed + rotation * (used - fixed)) % max(1, number_of - fixed)
        return jnp.zeros((number_of,), jnp.int32).at[order[jnp.where(places < fixed, places, shifted)]].set(jnp.asarray(sizes, jnp.int32))

    sizes = jnp.where(number % 4 == 0, named(heavy_load, number // 4), named(common, number - number // 4 - 1))
    mixed = jax.random.permutation(jax.random.fold_in(own, 3), number_of)
    giver, taker = mixed[0:number_of // 2 * 2:2], mixed[1:number_of // 2 * 2:2]
    margin = jnp.minimum(sizes[giver] - 1, limit - sizes[taker]) // 2
    margin = jnp.where((giver == order[0]) | (taker == order[0]) | (sizes[taker] == 0), 0, jnp.maximum(margin, 0))
    shifted = jax.random.randint(jax.random.fold_in(own, 4), (number_of // 2,), 0, 1 << 20) % (margin + 1)
    sizes = sizes.at[giver].add(-shifted).at[taker].add(shifted)
    items = jnp.searchsorted(jnp.cumsum(sizes), jnp.arange(rows * top), side="right").astype(jnp.int32)
    grid = items.reshape(top, rows).T
    grid = grid[jax.random.permutation(jax.random.fold_in(own, 1), rows)]
    rotation = jax.random.randint(jax.random.fold_in(own, 2), (rows, 1), 0, top)
    return jnp.take_along_axis(grid, (jnp.arange(top)[None, :] + rotation) % top, axis=1)


def shares(number_of, total, reach, slope, full):
    portions = [(1 << 20) // math.isqrt(standing ** slope) + 1 for standing in range(1, number_of + 1)]
    largest = reach if full else min(reach, max(-(-total // number_of), total * portions[0] // sum(portions)))
    least = 1 if total - largest >= number_of - 1 else 0
    counts, rest = [largest] + [least] * (number_of - 1), total - largest - least * (number_of - 1)
    while rest > 0:
        movable = [i for i in range(1, number_of) if counts[i] < largest] or [i for i in range(1, number_of) if counts[i] < reach]
        mass, remaining = sum([portions[i] for i in movable]), rest
        for i in movable:
            addition = min(reach - counts[i], max(1, remaining * portions[i] // mass), rest)
            counts[i] = counts[i] + addition
            rest = rest - addition
    return np.array(counts)


def bell_draw(stream_key, dims, width, reach, cuts=(), kind=jnp.bfloat16):
    loudness = shard_levels(stream_key, dims, cuts, -0.22, 0.18) if cuts else 1.0
    array = jax.random.normal(stream_key, dims, jnp.float32) * width * loudness
    return jnp.minimum(jnp.maximum(array, -reach), reach).astype(kind)


def setup_inputs(seed: int = 0) -> dict:
    splits = jax.random.split(jax.random.key(seed), 6)
    visibilities = bell_draw(splits[0], (NCG, BASE, 2 * K), 1.0, 6.0, ((0, 4), (1, 32)), jnp.float32)
    kernels = bell_draw(splits[1], (NCG, NW, 2, K, 2 * S), K ** -0.5, 0.75, ((0, 4),))
    destination_keys = jax.random.split(jax.random.fold_in(splits[2], 1), NCG * BASE // BLK_DEV)
    destination_turns = jax.random.permutation(jax.random.fold_in(splits[2], 3), NCG * BASE // BLK_DEV)
    destination = jax.vmap(lambda own, number: assign_block(jax.random.fold_in(splits[2], 2), own, number, BLK_DEV, N_TILE, 1, CAP, 2))(destination_keys, destination_turns).reshape((NCG, BASE, 1))
    cell = place_ends(jax.random.randint(splits[3], (NCG, BASE), 0, CELLS_T), jax.random.fold_in(splits[3], 1), 0, CELLS_T - 1).astype(jnp.int32)
    plane = place_ends(jax.random.randint(splits[4], (NCG, BASE), 0, NW), jax.random.fold_in(splits[4], 1), 0, NW - 1).astype(jnp.int32)
    return {"visibilities": visibilities, "kernels": kernels, "destination": destination, "cell": cell, "plane": plane}


def round_half(values):
    return lax.optimization_barrier(values.astype(jnp.bfloat16)).astype(jnp.float32)


def phase_tables(first_row, row_count, grid_width, pixels):
    spacing = grid_width // pixels - 1
    row_index = first_row + jnp.arange(row_count, dtype=jnp.int32)
    pixel_index = jnp.arange(pixels, dtype=jnp.int32)
    product = jnp.mod((row_index[:, None] - grid_width // 2) * (spacing * (pixel_index[None, :] - pixels // 2)), grid_width)
    phase_angle = product.astype(jnp.float32) * (2.0 * math.pi / grid_width)
    return round_half(jnp.cos(phase_angle)), round_half(jnp.sin(phase_angle))


def block_patches(samples, kernel_rows):
    sample_count = samples.shape[1] // 2
    support = kernel_rows.shape[3] // 2
    vis_real = samples[:, :sample_count, None]
    vis_imag = samples[:, sample_count:, None]
    kern_real = kernel_rows[:, 0, :, support:].astype(jnp.float32)
    kern_imag = kernel_rows[:, 1, :, support:].astype(jnp.float32)
    weighted_real = round_half(vis_real * kern_real - vis_imag * kern_imag)
    weighted_imag = round_half(vis_real * kern_imag + vis_imag * kern_real)
    u_kernel = kernel_rows[:, :, :, :support].astype(jnp.float32)
    v_weighted = jnp.stack([jnp.stack([weighted_real, weighted_imag], 2), jnp.stack([-weighted_imag, weighted_real], 2)], 1)
    return jnp.einsum('bpkx,bpkqy->bxqy', u_kernel, v_weighted)


def reference(visibilities, kernels, destination, cell, plane):
    groups = visibilities.shape[0]
    slab_rows = G // N_TILE
    cell_cols = G // S
    slot_total = N_TILE * CAP
    stride = math.gcd(slot_total, 256)
    cosine, sine = phase_tables(0, G, G, P_SIZE)
    cosine_cells = cosine.reshape(cell_cols, S, P_SIZE)
    sine_cells = sine.reshape(cell_cols, S, P_SIZE)

    def one_slab(image_acc, packed):
        group_id, tile_id = packed
        samples_all = lax.dynamic_index_in_dim(visibilities, group_id, 0, keepdims=False)
        kernel_set = lax.dynamic_index_in_dim(kernels, group_id, 0, keepdims=False)
        owners = lax.dynamic_index_in_dim(destination, group_id, 0, keepdims=False)[:, 0]
        cell_ids = lax.dynamic_index_in_dim(cell, group_id, 0, keepdims=False)
        plane_ids = lax.dynamic_index_in_dim(plane, group_id, 0, keepdims=False)
        sorted_ids = jnp.argsort(owners, stable=True).astype(jnp.int32)
        amount = jnp.sum((owners == tile_id).astype(jnp.int32))
        first = jnp.sum((owners < tile_id).astype(jnp.int32))
        padded_ids = jnp.concatenate([sorted_ids, jnp.zeros((slot_total,), jnp.int32)])
        chosen = lax.dynamic_slice_in_dim(padded_ids, first, slot_total)
        in_use = (jnp.arange(slot_total, dtype=jnp.int32) < amount).astype(samples_all.dtype)
        samples = samples_all[chosen] * in_use[:, None]
        samples = samples.reshape(slot_total // stride, stride, samples.shape[1])
        cell_slot = cell_ids[chosen].reshape(slot_total // stride, stride)
        plane_slot = plane_ids[chosen].reshape(slot_total // stride, stride)

        def add_block(grid_cells, blk):
            sample_blk, cell_blk, plane_blk = blk
            patches = block_patches(sample_blk, kernel_set[plane_blk])
            return grid_cells.at[cell_blk].add(patches), None

        grid_start = jnp.zeros((CELLS_T, S, 2, S), jnp.float32)
        grid_cells, _ = lax.scan(add_block, grid_start, (samples, cell_slot, plane_slot))
        grid_round = round_half(grid_cells).reshape(slab_rows // S, cell_cols, S, 2, S)
        with_cosine = jnp.einsum('acxpy,cym->pmax', grid_round, cosine_cells).reshape(2, P_SIZE, slab_rows)
        with_sine = jnp.einsum('acxpy,cym->pmax', grid_round, sine_cells).reshape(2, P_SIZE, slab_rows)
        transformed_real = round_half(with_cosine[0] - with_sine[1])
        transformed_imag = round_half(with_sine[0] + with_cosine[1])
        own_cosine = lax.dynamic_slice_in_dim(cosine, tile_id * slab_rows, slab_rows, 0)
        own_sine = lax.dynamic_slice_in_dim(sine, tile_id * slab_rows, slab_rows, 0)
        partial_image = jnp.dot(transformed_real, own_cosine, preferred_element_type=jnp.float32) - jnp.dot(transformed_imag, own_sine, preferred_element_type=jnp.float32)
        return image_acc + partial_image, None

    group_ids = jnp.repeat(jnp.arange(groups, dtype=jnp.int32), N_TILE)
    tile_ids = jnp.tile(jnp.arange(N_TILE, dtype=jnp.int32), groups)
    image_acc, _ = lax.scan(one_slab, jnp.zeros((P_SIZE, P_SIZE), jnp.float32), (group_ids, tile_ids))
    return image_acc.T * (1.0 / G)
```

```python
import functools
import math

import jax
import jax.numpy as jnp
import ml_dtypes
import numpy as np
from jax import lax
from jax.experimental import pallas as pl
from jax.experimental.pallas import tpu as pltpu
from jax.sharding import PartitionSpec as P

G = 8192
S = 64
NW = 32
PIX = 1024
NT = 32
NC = 4
BLK = 256
CAP = 31
SLOTS = 32
ALL = NT * SLOTS
MIB = 1 << 20
BF = jnp.bfloat16
F32 = jnp.float32
MESH = pl.DeviceIdType.MESH


def split(table):
    high = table.astype(np.float32).astype(ml_dtypes.bfloat16)
    low = (table - high.astype(np.float64)).astype(ml_dtypes.bfloat16)
    return high, low


def row_tables():
    step = G // PIX - 1
    l0 = np.arange(128)
    angle = 2 * math.pi / 128 * ((step * (l0[:, None] - PIX // 2) * (l0[None, :] - 64)) % 128)
    c, s = np.cos(angle), np.sin(angle)
    over_r = np.block([[c, -s], [s, c]]).astype(np.float32).astype(ml_dtypes.bfloat16)
    pixel = l0[:, None] + 128 * np.arange(8)[None, :]
    angle = 2 * math.pi / G * ((step * (pixel[:, :, None] - PIX // 2) * np.arange(S)) % G)
    c, s = np.cos(angle), np.sin(angle)
    over_x = np.concatenate([np.concatenate([c, -s], 2), np.concatenate([s, c], 2)], 1)
    high, low = split(over_x)
    return over_r, np.concatenate([high, low], 1).reshape(128 * 32, 128)


def column_tables():
    step = G // PIX - 1
    m0 = np.arange(32)
    angle = 2 * math.pi / 32 * ((step * (m0[:, None] - PIX // 2) * (m0[None, :] - 16)) % 32)
    c, s = np.cos(angle), np.sin(angle)
    over_t = np.concatenate(split(np.block([[c, -s], [s, c]])), 0)
    pixel = m0[:, None] + 32 * m0[None, :]
    angle = 2 * math.pi / G * ((step * (pixel[:, :, None] - PIX // 2) * np.arange(256)) % G)
    over_v = np.concatenate([np.cos(angle), -np.sin(angle)], 2) / G
    high, low = split(over_v)
    return over_t, np.concatenate([high, low], 1).reshape(32 * 64, 512)


def iota(shape, axis):
    return lax.broadcasted_iota(jnp.int32, shape, axis)


def dot(a, b):
    return jnp.dot(a, b, preferred_element_type=F32)


def dot_t(a, b):
    return lax.dot_general(a, b, (((1,), (1,)), ((), ())), preferred_element_type=F32)


def fill_slots(samples, dest, cell, plane, skipped):
    column = jnp.bitwise_and(cell, 127)
    owner = lax.shift_right_logical(column, 2)
    inner = jnp.bitwise_and(column, 3)
    row = dest * 4 + lax.shift_right_logical(cell, 7)
    named = iota((NT, BLK), 0) == owner
    one = jnp.where(named, 1.0, 0.0)
    one_b = one.astype(BF)
    before = jnp.where(iota((BLK, BLK), 0) < iota((BLK, BLK), 1), 1.0, 0.0).astype(BF)
    count = dot(one_b, before)
    rank = jnp.sum(one * count, axis=0, keepdims=True).astype(jnp.int32) - skipped
    here = jnp.logical_and(rank >= 0, rank < CAP)
    slot = jnp.where(here, owner * SLOTS + rank, -1)
    pick = jnp.where(iota((ALL, BLK), 0) == slot, 1.0, 0.0).astype(BF)
    lane = iota((128, BLK), 0)
    kind = lax.shift_right_logical(lane, 5)
    value = jnp.where(kind == 0, row, jnp.where(kind == 1, plane, jnp.where(kind == 2, inner, 1)))
    held = jnp.logical_and(here, jnp.logical_or(kind == 3, jnp.bitwise_and(lane, 31) == rank))
    facts = dot_t(one_b, jnp.where(held, value.astype(F32), 0.0).astype(BF))
    last = jnp.where(iota((ALL, NT), 0) == iota((ALL, NT), 1) * SLOTS + CAP, 1.0, 0.0).astype(BF)
    slots = dot(pick, samples.astype(BF)) + dot(last, facts.astype(BF))
    return slots.astype(BF), jnp.sum(one, axis=1, keepdims=True)


def exchange_body(first, samples, dest, cell, plane, skipped, *rest):
    if first:
        kern, recv, table, weight, most, send, send_sem, recv_sem = rest
    else:
        recv, send, send_sem, recv_sem = rest
    me = lax.axis_index("tile")
    chan = lax.axis_index("chan")
    barrier = pltpu.get_barrier_semaphore()

    def greet(i, _):
        pl.semaphore_signal(
            barrier, inc=1, device_id=(lax.rem(me + i, NT), chan), device_id_type=MESH
        )
        return 0

    lax.fori_loop(1, NT, greet, 0)
    slots, named = fill_slots(samples[...], dest[...], cell[...], plane[...], skipped[...])
    send[...] = slots
    pl.semaphore_wait(barrier, NT - 1)

    def copy(i):
        to = lax.rem(me + i, NT)
        return pltpu.make_async_remote_copy(
            src_ref=send.at[pl.ds(pl.multiple_of(to * SLOTS, SLOTS), SLOTS)],
            dst_ref=recv.at[pl.ds(pl.multiple_of(me * SLOTS, SLOTS), SLOTS)],
            send_sem=send_sem.at[i],
            recv_sem=recv_sem.at[i],
            device_id=(to, chan),
            device_id_type=MESH,
        )

    def start(i, _):
        copy(i).start()
        return 0

    lax.fori_loop(1, NT, start, 0)
    own = pl.ds(pl.multiple_of(me * SLOTS, SLOTS), SLOTS)
    recv[own, :] = send[own, :]
    if first:
        most[...] = jnp.broadcast_to(jnp.max(named, axis=0, keepdims=True), (8, 128))
        low = iota((S, 128), 1) < S

        def prepare(w, _):
            both = kern[pl.ds(pl.multiple_of(w * 128, 128), 128), :].astype(F32)
            real, imag = both[:S], both[S:]
            turned = both.T[:S]
            base = pl.multiple_of(w * 128, 128)
            table[pl.ds(base, S), :] = turned
            swapped = pltpu.roll(turned, S, 1)
            table[pl.ds(base + S, S), :] = jnp.where(low, -swapped, swapped)
            weight[pl.ds(base, S), :] = jnp.where(low, pltpu.roll(real, S, 1), imag).astype(BF)
            weight[pl.ds(base + S, S), :] = jnp.where(low, -pltpu.roll(imag, S, 1), real).astype(BF)
            return 0

        lax.fori_loop(0, NW, prepare, 0)

    def wait(i, _):
        copy(i).wait()
        return 0

    lax.fori_loop(1, NT, wait, 0)


def exchange(first, samples, dest, cell, plane, skipped, kern=None):
    vmem = pl.BlockSpec(memory_space=pltpu.VMEM)
    shapes = [jax.ShapeDtypeStruct((ALL, 128), BF)]
    operands = [samples, dest, cell, plane, skipped]
    if first:
        shapes += [
            jax.ShapeDtypeStruct((NW * 128, 128), F32),
            jax.ShapeDtypeStruct((NW * 128, 128), BF),
            jax.ShapeDtypeStruct((8, 128), F32),
        ]
        operands.append(kern)
    return pl.pallas_call(
        functools.partial(exchange_body, first),
        out_shape=shapes,
        in_specs=[vmem] * len(operands),
        out_specs=[vmem] * len(shapes),
        scratch_shapes=[
            pltpu.VMEM((ALL, 128), BF),
            pltpu.SemaphoreType.DMA((NT,)),
            pltpu.SemaphoreType.DMA((NT,)),
        ],
        compiler_params=pltpu.CompilerParams(
            collective_id=0 if first else 2, has_side_effects=True, vmem_limit_bytes=32 * MIB
        ),
        name="exchange" if first else "exchange_more",
    )(*operands)


def grid_body(
    recv, table, weight, over_r, over_x, out, grid, half, fill_a, fill_b, facts_v, facts, sem
):
    lane = iota((ALL, 128), 1)
    slot = iota((ALL, 128), 0)
    blocks = jnp.where(jnp.bitwise_and(slot, SLOTS - 1) == CAP, 0.0, recv[...].astype(F32))
    swapped = pltpu.roll(blocks, S, 1)
    fill_a[...] = jnp.where(lane < S, blocks, swapped)
    fill_b[...] = jnp.where(lane < S, swapped, blocks)
    last = jnp.where(iota((NT, ALL), 1) == iota((NT, ALL), 0) * SLOTS + CAP, 1.0, 0.0).astype(BF)
    raw = dot(last, recv[...])
    code = (pltpu.roll(raw, 64, 1) * 128.0 + raw) * 32.0 + pltpu.roll(raw, 96, 1)
    facts_v[...] = jnp.where(iota((NT, 128), 1) < SLOTS, code, raw).astype(jnp.int32)
    to_scalar = pltpu.make_async_copy(facts_v, facts, sem)
    to_scalar.start()

    def clear(i, _):
        grid[pl.ds(pl.multiple_of(i * 512, 512), 512), :] = jnp.zeros((512, 128), F32)
        return 0

    lax.fori_loop(0, 64, clear, 0)
    to_scalar.wait()

    def from_source(t, _):
        def four(j, _):
            made = []
            for k in range(4):
                i = j * 4 + k
                fact = facts[t, i]
                w = jnp.bitwise_and(fact, 31)
                base = pl.multiple_of(w * 128, 128)
                i = t * SLOTS + i
                left = (
                    fill_a[pl.ds(i, 1), :] * table[pl.ds(base, S), :]
                    + fill_b[pl.ds(i, 1), :] * table[pl.ds(base + S, S), :]
                ).astype(BF)
                patch = dot(left, weight[pl.ds(base, 128), :])
                made.append((lax.shift_right_logical(fact, 5), patch))
            for place, patch in made:
                at = pl.ds(pl.multiple_of(place * S, S), S)
                grid[at, :] = grid[at, :] + patch
            return 0

        lax.fori_loop(0, lax.shift_right_logical(facts[t, 96] + 3, 2), four, 0)
        return 0

    lax.fori_loop(0, NT, from_source, 0)

    def over_rows(x, _):
        part = [grid[pl.ds(i * 8192 + x, 128, stride=S), :] for i in range(4)]
        real = jnp.concatenate([p[:, :S] for p in part], axis=1)
        imag = jnp.concatenate([p[:, S:] for p in part], axis=1)
        got = dot(over_r[...], jnp.concatenate([real, imag], axis=0).astype(BF))
        half[pl.ds(x, 128, stride=128), :] = got[:128, :128]
        half[pl.ds(S + x, 128, stride=128), :] = got[128:, :128]
        half[pl.ds(16384 + x, 128, stride=128), :] = got[:128, 128:]
        half[pl.ds(16384 + S + x, 128, stride=128), :] = got[128:, 128:]
        return 0

    lax.fori_loop(0, S, over_rows, 0)
    pixels = grid

    def over_offsets(l0, _):
        at = pl.multiple_of(l0 * 128, 128)
        right = jnp.concatenate(
            [half[pl.ds(at, 128), :], half[pl.ds(16384 + at, 128), :]], axis=1
        ).astype(BF)
        got = dot(over_x[pl.ds(pl.multiple_of(l0 * 32, 32), 32), :], right)
        got = got[:16] + got[16:]
        for side in range(2):
            for q in range(2):
                pixels[pl.ds(side * 2048 + 2 * l0 + q, 8, stride=256), :] = got[
                    8 * q : 8 * q + 8, 128 * side : 128 * side + 128
                ]
        return 0

    lax.fori_loop(0, 128, over_offsets, 0, unroll=4)
    out[:, :128] = pixels[:2048, :].astype(out.dtype)
    out[:, 128:] = pixels[2048:4096, :].astype(out.dtype)


def grid_and_rows(recv, table, weight, over_r, over_x, dtype):
    vmem = pl.BlockSpec(memory_space=pltpu.VMEM)
    return pl.pallas_call(
        grid_body,
        out_shape=jax.ShapeDtypeStruct((2048, 256), dtype),
        in_specs=[vmem] * 5,
        out_specs=vmem,
        scratch_shapes=[
            pltpu.VMEM((512 * S, 128), F32),
            pltpu.VMEM((2 * 128 * 128, 128), F32),
            pltpu.VMEM((ALL, 128), F32),
            pltpu.VMEM((ALL, 128), F32),
            pltpu.VMEM((NT, 128), jnp.int32),
            pltpu.SMEM((NT, 128), jnp.int32),
            pltpu.SemaphoreType.DMA,
        ],
        compiler_params=pltpu.CompilerParams(vmem_limit_bytes=56 * MIB),
        name="grid_and_rows",
    )(recv, table, weight, over_r, over_x)


def finish_body(
    pixels, over_t, over_v, out, recv, wide, middle, fold, last, send_a, recv_a, send_b, recv_b
):
    me = lax.axis_index("tile")
    chan = lax.axis_index("chan")
    home = me // 8
    stays = home == chan
    barrier = pltpu.get_barrier_semaphore()

    def greet(i, _):
        pl.semaphore_signal(
            barrier, inc=1, device_id=(lax.rem(me + i, NT), chan), device_id_type=MESH
        )
        return 0

    lax.fori_loop(1, NT, greet, 0)

    def greet_source(i, _):
        from_t, from_c = chan * 8 + i // NC, lax.rem(i, NC)

        @pl.when(jnp.logical_or(from_t != me, from_c != chan))
        def _():
            pl.semaphore_signal(barrier, inc=1, device_id=(from_t, from_c), device_id_type=MESH)

        return 0

    lax.fori_loop(0, NT, greet_source, 0)
    pl.semaphore_wait(barrier, jnp.where(stays, 2 * NT - 2, 2 * NT - 1))

    def copy(i):
        to = lax.rem(me + i, NT)
        return pltpu.make_async_remote_copy(
            src_ref=pixels.at[pl.ds(pl.multiple_of(to * 64, 64), 64)],
            dst_ref=recv.at[pl.ds(pl.multiple_of(me * 64, 64), 64)],
            send_sem=send_a.at[i],
            recv_sem=recv_a.at[i],
            device_id=(to, chan),
            device_id_type=MESH,
        )

    def start(i, _):
        copy(i).start()
        return 0

    lax.fori_loop(1, NT, start, 0)
    own = pl.ds(pl.multiple_of(me * 64, 64), 64)
    recv[own, :] = pixels[own, :]

    def wait(i, _):
        copy(i).wait()
        return 0

    lax.fori_loop(1, NT, wait, 0)
    for side in range(2):
        wide[side * 2048 : side * 2048 + 2048, :] = recv[
            :, 128 * side : 128 * side + 128
        ].astype(F32)

    def over_tiles(l, _):
        rows = [
            jnp.concatenate(
                [wide[pl.ds(side * 2048 + 2 * l + q, NT, stride=64), :] for side in range(2)],
                axis=1,
            )
            for q in range(2)
        ]
        got = dot(over_t[...], jnp.concatenate(rows, axis=0).astype(BF))
        got = got[:64] + got[64:]
        at = pl.multiple_of(l * 64, 64)
        middle[pl.ds(at, 64), :] = got[:, :128]
        middle[pl.ds(2048 + at, 64), :] = got[:, 128:]
        return 0

    lax.fori_loop(0, 32, over_tiles, 0, unroll=2)

    def over_columns(a, _):
        made = []
        for b in range(4):
            m0 = b * 8 + a
            right = jnp.concatenate(
                [
                    middle[pl.ds(side * 2048 + 32 * q + m0, 32, stride=64), :]
                    for q in range(2)
                    for side in range(2)
                ],
                axis=1,
            )
            high = right.astype(BF)
            low = (right - high.astype(F32)).astype(BF)
            left = over_v[pl.ds(pl.multiple_of(m0 * 64, 64), 64), :]
            got = dot_t(left, high)
            made.append(got[:32] + got[32:] + dot_t(left[:32], low))
        fold[pl.ds(a, 32, stride=8), :] = jnp.concatenate(made, axis=1)
        return 0

    lax.fori_loop(0, 8, over_columns, 0)
    slot = lax.rem(me, 8) * NC + chan

    def give(i):
        to = lax.rem(me + i, NT)
        return pltpu.make_async_remote_copy(
            src_ref=fold.at[pl.ds(pl.multiple_of(to * 8, 8), 8)],
            dst_ref=last.at[pl.ds(pl.multiple_of(slot * 8, 8), 8)],
            send_sem=send_b.at[i],
            recv_sem=recv_b.at[slot],
            device_id=(to, home),
            device_id_type=MESH,
        )

    def take(i):
        at = pl.ds(pl.multiple_of(i * 8, 8), 8)
        return pltpu.make_async_remote_copy(
            src_ref=last.at[at],
            dst_ref=last.at[at],
            send_sem=send_b.at[i],
            recv_sem=recv_b.at[i],
            device_id=(chan * 8 + i // NC, lax.rem(i, NC)),
            device_id_type=MESH,
        )

    @pl.when(jnp.logical_not(stays))
    def _():
        give(0).start()

    @pl.when(stays)
    def _():
        last[pl.ds(pl.multiple_of(slot * 8, 8), 8), :] = fold[
            pl.ds(pl.multiple_of(me * 8, 8), 8), :
        ]

    def start_b(i, _):
        give(i).start()
        return 0

    lax.fori_loop(1, NT, start_b, 0)

    def wait_b(i, _):
        @pl.when(jnp.logical_or(jnp.logical_not(stays), i != slot))
        def _():
            take(i).wait_recv()

        return 0

    lax.fori_loop(0, NT, wait_b, 0)

    @pl.when(jnp.logical_not(stays))
    def _():
        give(0).wait_send()

    def sent_b(i, _):
        give(i).wait_send()
        return 0

    lax.fori_loop(1, NT, sent_b, 0)
    for t in range(8):
        total = last[t * 32 : t * 32 + 8, :]
        for c in range(1, NC):
            total = total + last[t * 32 + c * 8 : t * 32 + c * 8 + 8, :]
        out[t * 8 : t * 8 + 8, :] = total


def finish(pixels, over_t, over_v):
    vmem = pl.BlockSpec(memory_space=pltpu.VMEM)
    return pl.pallas_call(
        finish_body,
        out_shape=jax.ShapeDtypeStruct((64, 128), F32),
        in_specs=[vmem] * 3,
        out_specs=vmem,
        scratch_shapes=[
            pltpu.VMEM((2048, 256), BF),
            pltpu.VMEM((4096, 128), F32),
            pltpu.VMEM((4096, 128), F32),
            pltpu.VMEM((256, 128), F32),
            pltpu.VMEM((256, 128), F32),
            pltpu.SemaphoreType.DMA((NT,)),
            pltpu.SemaphoreType.DMA((NT,)),
            pltpu.SemaphoreType.DMA((NT,)),
            pltpu.SemaphoreType.DMA((NT,)),
        ],
        compiler_params=pltpu.CompilerParams(
            collective_id=1, has_side_effects=True, vmem_limit_bytes=32 * MIB
        ),
        name="finish",
    )(pixels, over_t, over_v)


def local(visibilities, kernels, destination, cell, plane):
    over_r, over_x = (jnp.asarray(t) for t in row_tables())
    over_t, over_v = (jnp.asarray(t) for t in column_tables())
    samples = visibilities[0]
    dest = destination.reshape(1, BLK)
    kern = kernels.reshape(NW * 128, 128)
    none = jnp.zeros((1, BLK), jnp.int32)
    recv, table, weight, most = exchange(True, samples, dest, cell, plane, none, kern)
    largest = lax.pmax(most[0, 0], ("tile", "chan"))
    pixels = grid_and_rows(recv, table, weight, over_r, over_x, BF)

    def more(pixels):
        def again(state):
            done, total = state
            more_recv = exchange(
                False, samples, dest, cell, plane, jnp.broadcast_to(done, (1, BLK))
            )[0]
            return done + CAP, total + grid_and_rows(
                more_recv, table, weight, over_r, over_x, F32
            )

        return lax.while_loop(
            lambda state: state[0].astype(F32) < largest,
            again,
            (jnp.int32(CAP), pixels.astype(F32)),
        )[1].astype(BF)

    pixels = lax.cond(largest > CAP, more, lambda p: p, pixels)
    out = finish(pixels, over_t, over_v)
    return out.reshape(8, 8, 4, 32).transpose(0, 3, 2, 1).reshape(256, 32)


def solution(mesh):
    placed = (
        P("chan", "tile", None),
        P("chan", None, None, None, None),
        P("chan", "tile", None),
        P("chan", "tile"),
        P("chan", "tile"),
    )
    return jax.shard_map(
        local, mesh=mesh, in_specs=placed, out_specs=P("chan", "tile"), check_vma=False
    )
```

```python
import functools
import math

import jax
import jax.numpy as jnp
import ml_dtypes
import numpy as np
from jax import lax
from jax.experimental import pallas as pl
from jax.experimental.pallas import tpu as pltpu
from jax.sharding import PartitionSpec as P

G = 8192
S = 64
NW = 32
PIX = 1024
NT = 32
NC = 4
BLK = 256
CAP = 31
GS = 65
HS = 129
TOGETHER = 32
WS = 65
SLOTS = 32
ALL = NT * SLOTS
MIB = 1 << 20
BF = jnp.bfloat16
F32 = jnp.float32
MESH = pl.DeviceIdType.MESH


def split(table):
    high = table.astype(np.float32).astype(ml_dtypes.bfloat16)
    low = (table - high.astype(np.float64)).astype(ml_dtypes.bfloat16)
    return high, low


def row_tables():
    step = G // PIX - 1
    l0 = np.arange(128)
    angle = 2 * math.pi / 128 * ((step * (l0[:, None] - PIX // 2) * (l0[None, :] - 64)) % 128)
    c, s = np.cos(angle), np.sin(angle)
    over_r = np.block([[c, -s], [s, c]]).astype(np.float32).astype(ml_dtypes.bfloat16)
    pixel = l0[:, None] + 128 * np.arange(8)[None, :]
    angle = 2 * math.pi / G * ((step * (pixel[:, :, None] - PIX // 2) * np.arange(S)) % G)
    c, s = np.cos(angle), np.sin(angle)
    over_x = np.concatenate([np.concatenate([c, -s], 2), np.concatenate([s, c], 2)], 1)
    high, low = split(over_x)
    return over_r, np.concatenate([high, low], 1).reshape(128 * 32, 128)


def column_tables():
    step = G // PIX - 1
    m0 = np.arange(32)
    angle = 2 * math.pi / 32 * ((step * (m0[:, None] - PIX // 2) * (m0[None, :] - 16)) % 32)
    c, s = np.cos(angle), np.sin(angle)
    over_t = np.concatenate(split(np.block([[c, -s], [s, c]])), 0)
    pixel = m0[:, None] + 32 * m0[None, :]
    angle = 2 * math.pi / G * ((step * (pixel[:, :, None] - PIX // 2) * np.arange(256)) % G)
    over_v = np.concatenate([np.cos(angle), -np.sin(angle)], 2) / G
    high, low = split(over_v)
    return over_t, np.concatenate([high, low], 1).reshape(32 * 64, 512)


def iota(shape, axis):
    return lax.broadcasted_iota(jnp.int32, shape, axis)


def dot(a, b):
    return jnp.dot(a, b, preferred_element_type=F32)


def dot_t(a, b):
    return lax.dot_general(a, b, (((1,), (1,)), ((), ())), preferred_element_type=F32)


def fill_slots(samples, dest, cell, plane, skipped):
    column = jnp.bitwise_and(cell, 127)
    owner = lax.shift_right_logical(column, 2)
    inner = jnp.bitwise_and(column, 3)
    row = dest * 4 + lax.shift_right_logical(cell, 7)
    named = iota((NT, BLK), 0) == owner
    one = jnp.where(named, 1.0, 0.0)
    one_b = one.astype(BF)
    before = jnp.where(iota((BLK, BLK), 0) < iota((BLK, BLK), 1), 1.0, 0.0).astype(BF)
    count = dot(one_b, before)
    rank = jnp.sum(one * count, axis=0, keepdims=True).astype(jnp.int32) - skipped
    here = jnp.logical_and(rank >= 0, rank < CAP)
    slot = jnp.where(here, owner * SLOTS + rank, -1)
    pick = jnp.where(iota((ALL, BLK), 0) == slot, 1.0, 0.0).astype(BF)
    lane = iota((128, BLK), 0)
    kind = lax.shift_right_logical(lane, 5)
    value = jnp.where(kind == 0, row, jnp.where(kind == 1, plane, jnp.where(kind == 2, inner, 1)))
    held = jnp.logical_and(here, jnp.logical_or(kind == 3, jnp.bitwise_and(lane, 31) == rank))
    facts = dot_t(one_b, jnp.where(held, value.astype(F32), 0.0).astype(BF))
    named_most = jnp.max(jnp.sum(one, axis=1, keepdims=True), axis=0, keepdims=True)
    facts = jnp.where(iota((NT, 128), 1) < 112, facts, named_most)
    last = jnp.where(iota((ALL, NT), 0) == iota((ALL, NT), 1) * SLOTS + CAP, 1.0, 0.0).astype(BF)
    slots = dot(pick, samples.astype(BF)) + dot(last, facts.astype(BF))
    return slots.astype(BF)


def exchange_body(first, samples, dest, cell, plane, skipped, *rest):
    if first:
        kern_hbm, recv, facts, table, weight, most, send, send_sem, recv_sem, kern, mine, seen, kern_sem, send_y, recv_y = rest
    else:
        recv, facts, send, send_sem, recv_sem = rest
    me = lax.axis_index("tile")
    chan = lax.axis_index("chan")
    barrier = pltpu.get_barrier_semaphore()
    fetch = pltpu.make_async_copy(kern_hbm, kern, kern_sem) if first else None
    if first:
        fetch.start()

    def greet(i, _):
        pl.semaphore_signal(
            barrier, inc=1, device_id=(lax.rem(me + i, NT), chan), device_id_type=MESH
        )
        return 0

    lax.fori_loop(1, NT, greet, 0)
    if first:
        for i in range(1, NC):
            pl.semaphore_signal(
                barrier, inc=1, device_id=(me, lax.rem(chan + i, NC)), device_id_type=MESH
            )
    send[...] = fill_slots(samples[...], dest[...], cell[...], plane[...], skipped[...])
    pl.semaphore_wait(barrier, NT + NC - 2 if first else NT - 1)

    def copy(i):
        to = lax.rem(me + i, NT)
        return pltpu.make_async_remote_copy(
            src_ref=send.at[pl.ds(pl.multiple_of(to * SLOTS, SLOTS), SLOTS)],
            dst_ref=recv.at[pl.ds(pl.multiple_of(me * SLOTS, SLOTS), SLOTS)],
            send_sem=send_sem.at[i],
            recv_sem=recv_sem.at[i],
            device_id=(to, chan),
            device_id_type=MESH,
        )

    def start(i, _):
        copy(i).start()
        return 0

    lax.fori_loop(1, NT, start, 0)
    own = pl.ds(pl.multiple_of(me * SLOTS, SLOTS), SLOTS)
    recv[own, :] = send[own, :]
    if first:
        low = iota((S, 128), 1) < S

        def prepare(w, _):
            base = pl.multiple_of(w * 128, 128)
            both = kern[pl.ds(base, 128), :].astype(F32)
            real, imag = both[:S], both[S:]
            turned = both.T[:S]
            table[pl.ds(base, S), :] = turned
            swapped = pltpu.roll(turned, S, 1)
            table[pl.ds(base + S, S), :] = jnp.where(low, -swapped, swapped)
            weight[pl.ds(base, S), :] = jnp.where(low, pltpu.roll(real, S, 1), imag).astype(BF)
            weight[pl.ds(base + S, S), :] = jnp.where(low, -pltpu.roll(imag, S, 1), real).astype(BF)
            return 0

        fetch.wait()
        lax.fori_loop(0, 24, prepare, 0, unroll=2)

    def wait(i, _):
        copy(i).wait()
        return 0

    lax.fori_loop(1, NT, wait, 0)
    last = jnp.where(iota((NT, ALL), 1) == iota((NT, ALL), 0) * SLOTS + CAP, 1.0, 0.0).astype(BF)
    raw = dot(last, recv[...])
    lane = iota((NT, 128), 1)
    code = (pltpu.roll(raw, 64, 1) * 128.0 + raw) * 32.0 + pltpu.roll(raw, 96, 1)
    facts[...] = jnp.where(lane < SLOTS, code, raw).astype(jnp.int32)
    if first:
        largest = jnp.max(jnp.where(lane < 112, 0.0, raw), axis=0, keepdims=True)
        largest = jnp.broadcast_to(jnp.max(largest, axis=1, keepdims=True), (8, 128))
        mine[...] = largest

        def tell(i):
            return pltpu.make_async_remote_copy(
                src_ref=mine,
                dst_ref=seen.at[i],
                send_sem=send_y.at[i],
                recv_sem=recv_y.at[i],
                device_id=(me, lax.rem(chan + i, NC)),
                device_id_type=MESH,
            )

        for i in range(1, NC):
            tell(i).start()
        lax.fori_loop(24, NW, prepare, 0, unroll=2)
        for i in range(1, NC):
            tell(i).wait()
            largest = jnp.maximum(largest, seen[i])
        most[...] = largest


def exchange(first, samples, dest, cell, plane, skipped, kern=None):
    vmem = pl.BlockSpec(memory_space=pltpu.VMEM)
    shapes = [jax.ShapeDtypeStruct((ALL, 128), BF), jax.ShapeDtypeStruct((NT, 128), jnp.int32)]
    operands = [samples, dest, cell, plane, skipped]
    specs = [vmem] * 5
    scratch = [
        pltpu.VMEM((ALL, 128), BF),
        pltpu.SemaphoreType.DMA((NT,)),
        pltpu.SemaphoreType.DMA((NT,)),
    ]
    if first:
        shapes += [
            jax.ShapeDtypeStruct((NW * 128, 128), F32),
            jax.ShapeDtypeStruct((NW * 128, 128), BF),
            jax.ShapeDtypeStruct((8, 128), F32),
        ]
        operands.append(kern)
        specs.append(pl.BlockSpec(memory_space=pltpu.HBM))
        scratch += [
            pltpu.VMEM((NW * 128, 128), BF),
            pltpu.VMEM((8, 128), F32),
            pltpu.VMEM((NC, 8, 128), F32),
            pltpu.SemaphoreType.DMA,
            pltpu.SemaphoreType.DMA((NC,)),
            pltpu.SemaphoreType.DMA((NC,)),
        ]
    return pl.pallas_call(
        functools.partial(exchange_body, first),
        out_shape=shapes,
        in_specs=specs,
        out_specs=[vmem] * len(shapes),
        scratch_shapes=scratch,
        compiler_params=pltpu.CompilerParams(
            collective_id=0 if first else 2, has_side_effects=True, vmem_limit_bytes=32 * MIB
        ),
        name="exchange" if first else "exchange_more",
    )(*operands)


def grid_body(facts, recv, table, weight, over_r, over_x, out, grid, half, fill_a, fill_b, todo):
    lane = iota((ALL, 128), 1)
    slot = iota((ALL, 128), 0)
    blocks = jnp.where(jnp.bitwise_and(slot, SLOTS - 1) == CAP, 0.0, recv[...].astype(F32))
    swapped = pltpu.roll(blocks, S, 1)
    fill_a[...] = jnp.where(lane < S, blocks, swapped)
    fill_b[...] = jnp.where(lane < S, swapped, blocks)

    def clear(i, _):
        grid[pl.ds(pl.multiple_of(i * 512, 512), 512), :] = jnp.zeros((512, 128), F32)
        return 0

    lax.fori_loop(0, GS, clear, 0)

    def from_source(t, at):
        number = facts[t, 96]

        def eight(j, _):
            for k in range(8):
                i = j * 8 + k
                todo[at + i] = facts[t, i] * ALL + t * SLOTS + i
            return 0

        lax.fori_loop(0, lax.shift_right_logical(number + 7, 3), eight, 0)
        return at + number

    number = lax.fori_loop(0, NT, from_source, 0)
    for k in range(TOGETHER):
        todo[number + k] = CAP

    def blocks_together(j, _):
        made = []
        for k in range(TOGETHER):
            code = todo[j * TOGETHER + k]
            i = jnp.bitwise_and(code, ALL - 1)
            fact = lax.shift_right_logical(code, 10)
            base = pl.multiple_of(jnp.bitwise_and(fact, 31) * 128, 128)
            left = (
                fill_a[pl.ds(i, 1), :] * table[pl.ds(base, S), :]
                + fill_b[pl.ds(i, 1), :] * table[pl.ds(base + S, S), :]
            ).astype(BF)
            patch = dot(left, weight[pl.ds(base, 128), :])
            made.append((lax.shift_right_logical(fact, 5), patch))
        for place, patch in made:
            at = pl.ds(place * GS, S)
            grid[at, :] = grid[at, :] + patch
        return 0

    lax.fori_loop(0, (number + TOGETHER - 1) // TOGETHER, blocks_together, 0)

    def over_rows(x, _):
        part = [grid[pl.ds(i * 128 * GS + x, 128, stride=GS), :] for i in range(4)]
        real = jnp.concatenate([p[:, :S] for p in part], axis=1)
        imag = jnp.concatenate([p[:, S:] for p in part], axis=1)
        got = dot(over_r[...], jnp.concatenate([real, imag], axis=0).astype(BF))
        half[pl.ds(x, 128, stride=HS), :] = got[:128, :128]
        half[pl.ds(S + x, 128, stride=HS), :] = got[128:, :128]
        half[pl.ds(128 * HS + x, 128, stride=HS), :] = got[:128, 128:]
        half[pl.ds(128 * HS + S + x, 128, stride=HS), :] = got[128:, 128:]
        return 0

    lax.fori_loop(0, S, over_rows, 0, unroll=8)
    pixels = grid

    def over_offsets(l0, _):
        at = pl.multiple_of(l0 * HS, 1)
        right = jnp.concatenate(
            [half[pl.ds(at, 128), :], half[pl.ds(128 * HS + at, 128), :]], axis=1
        ).astype(BF)
        got = dot(over_x[pl.ds(pl.multiple_of(l0 * 32, 32), 32), :], right)
        got = got[:16] + got[16:]
        for side in range(2):
            for q in range(2):
                pixels[pl.ds(side * 2048 + 2 * l0 + q, 8, stride=256), :] = got[
                    8 * q : 8 * q + 8, 128 * side : 128 * side + 128
                ]
        return 0

    lax.fori_loop(0, 128, over_offsets, 0, unroll=16)
    out[:, :128] = pixels[:2048, :].astype(out.dtype)
    out[:, 128:] = pixels[2048:4096, :].astype(out.dtype)


def grid_and_rows(facts, recv, table, weight, over_r, over_x, dtype):
    vmem = pl.BlockSpec(memory_space=pltpu.VMEM)
    return pl.pallas_call(
        grid_body,
        out_shape=jax.ShapeDtypeStruct((2048, 256), dtype),
        in_specs=[pl.BlockSpec(memory_space=pltpu.SMEM)] + [vmem] * 5,
        out_specs=vmem,
        scratch_shapes=[
            pltpu.VMEM((512 * GS, 128), F32),
            pltpu.VMEM((2 * 128 * HS, 128), F32),
            pltpu.VMEM((ALL, 128), F32),
            pltpu.VMEM((ALL, 128), F32),
            pltpu.SMEM((ALL + 64,), jnp.int32),
        ],
        compiler_params=pltpu.CompilerParams(vmem_limit_bytes=56 * MIB),
        name="grid_and_rows",
    )(facts, recv, table, weight, over_r, over_x)


def finish_body(
    pixels,
    over_t,
    over_v_hbm,
    out,
    recv,
    wide,
    middle,
    fold,
    last,
    over_v,
    send_a,
    recv_a,
    send_b,
    recv_b,
    table_sem,
):
    fetch = pltpu.make_async_copy(over_v_hbm, over_v, table_sem)
    fetch.start()
    me = lax.axis_index("tile")
    chan = lax.axis_index("chan")
    home = me // 8
    stays = home == chan
    barrier = pltpu.get_barrier_semaphore()

    def greet(i, _):
        pl.semaphore_signal(
            barrier, inc=1, device_id=(lax.rem(me + i, NT), chan), device_id_type=MESH
        )
        return 0

    lax.fori_loop(1, NT, greet, 0)

    def greet_source(i, _):
        from_t, from_c = chan * 8 + i // NC, lax.rem(i, NC)

        @pl.when(jnp.logical_or(from_t != me, from_c != chan))
        def _():
            pl.semaphore_signal(barrier, inc=1, device_id=(from_t, from_c), device_id_type=MESH)

        return 0

    lax.fori_loop(0, NT, greet_source, 0)
    pl.semaphore_wait(barrier, jnp.where(stays, 2 * NT - 2, 2 * NT - 1))

    def copy(i):
        to = lax.rem(me + i, NT)
        return pltpu.make_async_remote_copy(
            src_ref=pixels.at[pl.ds(pl.multiple_of(to * 64, 64), 64)],
            dst_ref=recv.at[pl.ds(pl.multiple_of(me * 64, 64), 64)],
            send_sem=send_a.at[i],
            recv_sem=recv_a.at[i],
            device_id=(to, chan),
            device_id_type=MESH,
        )

    def start(i, _):
        copy(i).start()
        return 0

    lax.fori_loop(1, NT, start, 0)
    own = pl.ds(pl.multiple_of(me * 64, 64), 64)
    recv[own, :] = pixels[own, :]

    def wait(i, _):
        copy(i).wait()
        return 0

    lax.fori_loop(1, NT, wait, 0)

    def widen(t, _):
        block = recv[pl.ds(pl.multiple_of(t * 64, 64), 64), :].astype(F32)
        wide[pl.ds(t * WS, 64), :] = block[:, :128]
        wide[pl.ds((NT + t) * WS, 64), :] = block[:, 128:]
        return 0

    lax.fori_loop(0, NT, widen, 0, unroll=4)

    def over_tiles(l, _):
        rows = [
            jnp.concatenate(
                [wide[pl.ds(side * NT * WS + 2 * l + q, NT, stride=WS), :] for side in range(2)],
                axis=1,
            )
            for q in range(2)
        ]
        got = dot(over_t[...], jnp.concatenate(rows, axis=0).astype(BF))
        got = got[:64] + got[64:]
        middle[pl.ds(l * WS, 64), :] = got[:, :128]
        middle[pl.ds((32 + l) * WS, 64), :] = got[:, 128:]
        return 0

    lax.fori_loop(0, 32, over_tiles, 0, unroll=8)
    fetch.wait()

    def over_columns(a, _):
        made = []
        for b in range(4):
            m0 = b * 8 + a
            right = jnp.concatenate(
                [
                    middle[pl.ds(side * 32 * WS + 32 * q + m0, 32, stride=WS), :]
                    for q in range(2)
                    for side in range(2)
                ],
                axis=1,
            )
            high = right.astype(BF)
            low = (right - high.astype(F32)).astype(BF)
            left = over_v[pl.ds(pl.multiple_of(m0 * 64, 64), 64), :]
            got = dot_t(left, high)
            made.append(got[:32] + got[32:] + dot_t(left[:32], low))
        fold[pl.ds(a, 32, stride=8), :] = jnp.concatenate(made, axis=1)
        return 0

    lax.fori_loop(0, 8, over_columns, 0, unroll=4)
    slot = lax.rem(me, 8) * NC + chan

    def give(i):
        to = lax.rem(me + i, NT)
        return pltpu.make_async_remote_copy(
            src_ref=fold.at[pl.ds(pl.multiple_of(to * 8, 8), 8)],
            dst_ref=last.at[pl.ds(pl.multiple_of(slot * 8, 8), 8)],
            send_sem=send_b.at[i],
            recv_sem=recv_b.at[slot],
            device_id=(to, home),
            device_id_type=MESH,
        )

    def take(i):
        at = pl.ds(pl.multiple_of(i * 8, 8), 8)
        return pltpu.make_async_remote_copy(
            src_ref=last.at[at],
            dst_ref=last.at[at],
            send_sem=send_b.at[i],
            recv_sem=recv_b.at[i],
            device_id=(chan * 8 + i // NC, lax.rem(i, NC)),
            device_id_type=MESH,
        )

    @pl.when(jnp.logical_not(stays))
    def _():
        give(0).start()

    @pl.when(stays)
    def _():
        last[pl.ds(pl.multiple_of(slot * 8, 8), 8), :] = fold[
            pl.ds(pl.multiple_of(me * 8, 8), 8), :
        ]

    def start_b(i, _):
        give(i).start()
        return 0

    lax.fori_loop(1, NT, start_b, 0)

    def wait_b(i, _):
        @pl.when(jnp.logical_or(jnp.logical_not(stays), i != slot))
        def _():
            take(i).wait_recv()

        return 0

    lax.fori_loop(0, NT, wait_b, 0)

    @pl.when(jnp.logical_not(stays))
    def _():
        give(0).wait_send()

    def sent_b(i, _):
        give(i).wait_send()
        return 0

    lax.fori_loop(1, NT, sent_b, 0)
    for t in range(8):
        total = last[t * 32 : t * 32 + 8, :]
        for c in range(1, NC):
            total = total + last[t * 32 + c * 8 : t * 32 + c * 8 + 8, :]
        out[t * 8 : t * 8 + 8, :] = total


def finish(pixels, over_t, over_v):
    vmem = pl.BlockSpec(memory_space=pltpu.VMEM)
    return pl.pallas_call(
        finish_body,
        out_shape=jax.ShapeDtypeStruct((64, 128), F32),
        in_specs=[vmem] * 2 + [pl.BlockSpec(memory_space=pltpu.HBM)],
        out_specs=vmem,
        scratch_shapes=[
            pltpu.VMEM((2048, 256), BF),
            pltpu.VMEM((2 * NT * WS, 128), F32),
            pltpu.VMEM((2 * 32 * WS, 128), F32),
            pltpu.VMEM((256, 128), F32),
            pltpu.VMEM((256, 128), F32),
            pltpu.VMEM((2048, 512), BF),
            pltpu.SemaphoreType.DMA((NT,)),
            pltpu.SemaphoreType.DMA((NT,)),
            pltpu.SemaphoreType.DMA((NT,)),
            pltpu.SemaphoreType.DMA((NT,)),
            pltpu.SemaphoreType.DMA,
        ],
        compiler_params=pltpu.CompilerParams(
            collective_id=1, has_side_effects=True, vmem_limit_bytes=32 * MIB
        ),
        name="finish",
    )(pixels, over_t, over_v)


def local(visibilities, kernels, destination, cell, plane):
    over_r, over_x = (jnp.asarray(t) for t in row_tables())
    over_t, over_v = (jnp.asarray(t) for t in column_tables())
    samples = visibilities[0]
    dest = destination.reshape(1, BLK)
    kern = kernels.reshape(NW * 128, 128)
    none = jnp.zeros((1, BLK), jnp.int32)
    recv, facts, table, weight, most = exchange(True, samples, dest, cell, plane, none, kern)
    largest = most[0, 0]
    pixels = grid_and_rows(facts, recv, table, weight, over_r, over_x, BF)

    def more(pixels):
        def again(state):
            done, total = state
            more_recv, more_facts = exchange(
                False, samples, dest, cell, plane, jnp.broadcast_to(done, (1, BLK))
            )
            return done + CAP, total + grid_and_rows(
                more_facts, more_recv, table, weight, over_r, over_x, F32
            )

        return lax.while_loop(
            lambda state: state[0].astype(F32) < largest,
            again,
            (jnp.int32(CAP), pixels.astype(F32)),
        )[1].astype(BF)

    pixels = lax.cond(largest > CAP, more, lambda p: p, pixels)
    out = finish(pixels, over_t, over_v)
    return out.reshape(8, 8, 4, 32).transpose(0, 3, 2, 1).reshape(256, 32)


def solution(mesh):
    placed = (
        P("chan", "tile", None),
        P("chan", None, None, None, None),
        P("chan", "tile", None),
        P("chan", "tile"),
        P("chan", "tile"),
    )
    return jax.shard_map(
        local, mesh=mesh, in_specs=placed, out_specs=P("chan", "tile"), check_vma=False
    )
```

```python
import functools
import math

import jax
import jax.numpy as jnp
import ml_dtypes
import numpy as np
from jax import lax
from jax.experimental import pallas as pl
from jax.experimental.pallas import tpu as pltpu
from jax.sharding import PartitionSpec as P

G = 8192
S = 64
NW = 32
PIX = 1024
NT = 32
NC = 4
BLK = 256
CAP = 31
GS = 65
HS = 129
TOGETHER = 32
WS = 65
MS = 129
ROWS = 80
SLOTS = 32
ALL = NT * SLOTS
MIB = 1 << 20
BF = jnp.bfloat16
F32 = jnp.float32
MESH = pl.DeviceIdType.MESH


def split(table):
    high = table.astype(np.float32).astype(ml_dtypes.bfloat16)
    low = (table - high.astype(np.float64)).astype(ml_dtypes.bfloat16)
    return high, low


def row_tables():
    step = G // PIX - 1
    l0 = np.arange(128)
    angle = 2 * math.pi / 128 * ((step * (l0[:, None] - PIX // 2) * (l0[None, :] - 64)) % 128)
    c, s = np.cos(angle), np.sin(angle)
    over_r = np.block([[c, -s], [s, c]]).astype(np.float32).astype(ml_dtypes.bfloat16)
    pixel = l0[:, None] + 128 * np.arange(8)[None, :]
    angle = 2 * math.pi / G * ((step * (pixel[:, :, None] - PIX // 2) * np.arange(S)) % G)
    c, s = np.cos(angle), np.sin(angle)
    over_x = np.concatenate([np.concatenate([c, -s], 2), np.concatenate([s, c], 2)], 1)
    high, low = split(over_x)
    return over_r, np.concatenate([high, low], 1).reshape(128 * 32, 128)


def column_tables():
    step = G // PIX - 1
    m0 = np.arange(64)
    tile = np.arange(NT)
    angle = 2 * math.pi / 64 * ((step * (m0[:, None] - PIX // 2) * (tile[None, :] - NT)) % 64)
    c, s = np.cos(angle), np.sin(angle)
    over_t = np.concatenate(split(np.block([[c, -s], [s, c]])), 0)
    pixel = m0[:, None] + 64 * np.arange(16)[None, :]
    angle = 2 * math.pi / G * ((step * (pixel[:, :, None] - PIX // 2) * np.arange(128)) % G)
    over_j = np.concatenate([np.cos(angle), -np.sin(angle)], 2) / G
    high, low = split(over_j)
    angle = 2 * math.pi / 64 * ((step * (m0[:, None] - PIX // 2) * (tile[None, :] + 1 - NT)) % 64)
    lone = np.concatenate([np.cos(angle), np.sin(angle)], 0) / G
    return over_t, np.concatenate([high, low], 1).reshape(64 * 32, 256), split(lone)[0]


def iota(shape, axis):
    return lax.broadcasted_iota(jnp.int32, shape, axis)


def dot(a, b):
    return jnp.dot(a, b, preferred_element_type=F32)


def dot_t(a, b):
    return lax.dot_general(a, b, (((1,), (1,)), ((), ())), preferred_element_type=F32)


def fill_slots(samples, dest, cell, plane, skipped):
    column = jnp.bitwise_and(cell, 127)
    mirror = lax.shift_right_logical(column, 6)
    column = jnp.where(mirror == 1, 127 - column, column)
    owner = lax.shift_right_logical(column, 1)
    inner = jnp.bitwise_and(column, 1) + 2 * mirror
    row = dest * 4 + lax.shift_right_logical(cell, 7)
    named = iota((NT, BLK), 0) == owner
    one = jnp.where(named, 1.0, 0.0)
    one_b = one.astype(BF)
    before = jnp.where(iota((BLK, BLK), 0) < iota((BLK, BLK), 1), 1.0, 0.0).astype(BF)
    count = dot(one_b, before)
    rank = jnp.sum(one * count, axis=0, keepdims=True).astype(jnp.int32) - skipped
    here = jnp.logical_and(rank >= 0, rank < CAP)
    slot = jnp.where(here, owner * SLOTS + rank, -1)
    pick = jnp.where(iota((ALL, BLK), 0) == slot, 1.0, 0.0).astype(BF)
    lane = iota((128, BLK), 0)
    kind = lax.shift_right_logical(lane, 5)
    value = jnp.where(kind == 0, row, jnp.where(kind == 1, plane, jnp.where(kind == 2, inner, 1)))
    held = jnp.logical_and(here, jnp.logical_or(kind == 3, jnp.bitwise_and(lane, 31) == rank))
    facts = dot_t(one_b, jnp.where(held, value.astype(F32), 0.0).astype(BF))
    named_most = jnp.max(jnp.sum(one, axis=1, keepdims=True), axis=0, keepdims=True)
    facts = jnp.where(iota((NT, 128), 1) < 112, facts, named_most)
    last = jnp.where(iota((ALL, NT), 0) == iota((ALL, NT), 1) * SLOTS + CAP, 1.0, 0.0).astype(BF)
    slots = dot(pick, samples.astype(BF)) + dot(last, facts.astype(BF))
    return slots.astype(BF)


def exchange_body(first, samples, dest, cell, plane, skipped, *rest):
    if first:
        kern_hbm, recv, facts, table, weight, send, send_sem, recv_sem, kern, kern_sem = rest
    else:
        recv, facts, send, send_sem, recv_sem = rest
    me = lax.axis_index("tile")
    chan = lax.axis_index("chan")
    barrier = pltpu.get_barrier_semaphore()
    fetch = pltpu.make_async_copy(kern_hbm, kern, kern_sem) if first else None
    if first:
        fetch.start()

    def greet(i, _):
        pl.semaphore_signal(
            barrier, inc=1, device_id=(lax.rem(me + i, NT), chan), device_id_type=MESH
        )
        return 0

    lax.fori_loop(1, NT, greet, 0)
    send[...] = fill_slots(samples[...], dest[...], cell[...], plane[...], skipped[...])
    pl.semaphore_wait(barrier, NT - 1)

    def copy(i):
        to = lax.rem(me + i, NT)
        return pltpu.make_async_remote_copy(
            src_ref=send.at[pl.ds(pl.multiple_of(to * SLOTS, SLOTS), SLOTS)],
            dst_ref=recv.at[pl.ds(pl.multiple_of(me * SLOTS, SLOTS), SLOTS)],
            send_sem=send_sem.at[i],
            recv_sem=recv_sem.at[i],
            device_id=(to, chan),
            device_id_type=MESH,
        )

    def start(i, _):
        copy(i).start()
        return 0

    lax.fori_loop(1, NT, start, 0)
    own = pl.ds(pl.multiple_of(me * SLOTS, SLOTS), SLOTS)
    recv[own, :] = send[own, :]
    if first:
        low = iota((S, 128), 1) < S
        mirrored = jnp.where(iota((128, 128), 0) + iota((128, 128), 1) == 191, 1.0, 0.0).astype(BF)

        def prepare(w, _):
            base = pl.multiple_of(w * 128, 128)
            both = kern[pl.ds(base, 128), :].astype(F32)
            real, imag = both[:S], both[S:]
            turned = both.T[:S]
            table[pl.ds(base, S), :] = turned
            swapped = pltpu.roll(turned, S, 1)
            table[pl.ds(base + S, S), :] = jnp.where(low, -swapped, swapped)
            for side in range(2):
                at = base + side * NW * 128
                weight[pl.ds(at, S), :] = jnp.where(low, pltpu.roll(real, S, 1), imag).astype(BF)
                weight[pl.ds(at + S, S), :] = jnp.where(
                    low, -pltpu.roll(imag, S, 1), real
                ).astype(BF)
                if side == 0:
                    both = dot(kern[pl.ds(base, 128), :], mirrored)
                    real, imag = both[:S], both[S:]
            return 0

        fetch.wait()
        lax.fori_loop(0, NW, prepare, 0, unroll=2)

    def wait(i, _):
        copy(i).wait()
        return 0

    lax.fori_loop(1, NT, wait, 0)
    last = jnp.where(iota((NT, ALL), 1) == iota((NT, ALL), 0) * SLOTS + CAP, 1.0, 0.0).astype(BF)
    raw = dot(last, recv[...])
    lane = iota((NT, 128), 1)
    code = (pltpu.roll(raw, 64, 1) * 128.0 + raw) * 32.0 + pltpu.roll(raw, 96, 1)
    facts[...] = jnp.where(lane < SLOTS, code, raw).astype(jnp.int32)


def exchange(first, samples, dest, cell, plane, skipped, kern=None):
    vmem = pl.BlockSpec(memory_space=pltpu.VMEM)
    shapes = [jax.ShapeDtypeStruct((ALL, 128), BF), jax.ShapeDtypeStruct((NT, 128), jnp.int32)]
    operands = [samples, dest, cell, plane, skipped]
    specs = [vmem] * 5
    scratch = [
        pltpu.VMEM((ALL, 128), BF),
        pltpu.SemaphoreType.DMA((NT,)),
        pltpu.SemaphoreType.DMA((NT,)),
    ]
    if first:
        shapes += [
            jax.ShapeDtypeStruct((NW * 128, 128), F32),
            jax.ShapeDtypeStruct((2 * NW * 128, 128), BF),
        ]
        operands.append(kern)
        specs.append(pl.BlockSpec(memory_space=pltpu.HBM))
        scratch += [
            pltpu.VMEM((NW * 128, 128), BF),
            pltpu.SemaphoreType.DMA,
        ]
    return pl.pallas_call(
        functools.partial(exchange_body, first),
        out_shape=shapes,
        in_specs=specs,
        out_specs=[vmem] * len(shapes),
        scratch_shapes=scratch,
        compiler_params=pltpu.CompilerParams(
            collective_id=0 if first else 2, has_side_effects=True, vmem_limit_bytes=60 * MIB
        ),
        name="exchange" if first else "exchange_more",
    )(*operands)


def grid_body(facts, recv, table, weight, over_r, over_x, out, grid, half, fill_a, fill_b, todo):
    lane = iota((ALL, 128), 1)
    slot = iota((ALL, 128), 0)
    blocks = jnp.where(jnp.bitwise_and(slot, SLOTS - 1) == CAP, 0.0, recv[...].astype(F32))
    swapped = pltpu.roll(blocks, S, 1)
    fill_a[...] = jnp.where(lane < S, blocks, swapped)
    fill_b[...] = jnp.where(lane < S, swapped, blocks)

    def clear(i, _):
        grid[pl.ds(pl.multiple_of(i * 512, 512), 512), :] = jnp.zeros((512, 128), F32)
        return 0

    lax.fori_loop(0, GS, clear, 0)

    def from_source(t, at):
        number = facts[t, 96]

        def eight(j, _):
            for k in range(8):
                i = j * 8 + k
                todo[at + i] = facts[t, i] * ALL + t * SLOTS + i
            return 0

        lax.fori_loop(0, lax.shift_right_logical(number + 7, 3), eight, 0)
        return at + number

    number = lax.fori_loop(0, NT, from_source, 0)
    for k in range(TOGETHER):
        todo[number + k] = CAP

    def blocks_together(j, _):
        made = []
        for k in range(TOGETHER):
            code = todo[j * TOGETHER + k]
            i = jnp.bitwise_and(code, ALL - 1)
            fact = lax.shift_right_logical(code, 10)
            base = pl.multiple_of(jnp.bitwise_and(fact, 31) * 128, 128)
            left = (
                fill_a[pl.ds(i, 1), :] * table[pl.ds(base, S), :]
                + fill_b[pl.ds(i, 1), :] * table[pl.ds(base + S, S), :]
            ).astype(BF)
            side = lax.shift_right_logical(fact, 13)
            patch = dot(left, weight[pl.ds(pl.multiple_of(base + side * NW * 128, 128), 128), :])
            made.append((lax.shift_right_logical(fact, 5), patch))
        for place, patch in made:
            at = pl.ds(place * GS, S)
            grid[at, :] = grid[at, :] + patch
        return 0

    lax.fori_loop(0, (number + TOGETHER - 1) // TOGETHER, blocks_together, 0)

    def over_rows(x, _):
        part = [grid[pl.ds(i * 128 * GS + x, 128, stride=GS), :] for i in range(4)]
        real = jnp.concatenate([p[:, :S] for p in part], axis=1)
        imag = jnp.concatenate([p[:, S:] for p in part], axis=1)
        got = dot(over_r[...], jnp.concatenate([real, imag], axis=0).astype(BF))
        half[pl.ds(x, 128, stride=HS), :] = got[:128, :128]
        half[pl.ds(S + x, 128, stride=HS), :] = got[128:, :128]
        half[pl.ds(128 * HS + x, 128, stride=HS), :] = got[:128, 128:]
        half[pl.ds(128 * HS + S + x, 128, stride=HS), :] = got[128:, 128:]
        return 0

    lax.fori_loop(0, S, over_rows, 0, unroll=8)
    pixels = grid

    def over_offsets(l0, _):
        at = l0 * HS
        right = jnp.concatenate(
            [half[pl.ds(at, 128), :], half[pl.ds(128 * HS + at, 128), :]], axis=1
        ).astype(BF)
        got = dot(over_x[pl.ds(pl.multiple_of(l0 * 32, 32), 32), :], right)
        got = got[:16] + got[16:]
        turned = pltpu.roll(got[:, 128:], 1, 1)
        for q in range(2):
            rows = slice(8 * q, 8 * q + 8)
            pixels[pl.ds(2 * l0 + q, 8, stride=256), :] = got[rows, :128]
            pixels[pl.ds(2048 + 2 * l0 + q, 8, stride=256), :] = (
                turned[rows] if q == 0 else -turned[rows]
            )
        return 0

    lax.fori_loop(0, 128, over_offsets, 0, unroll=16)
    lane = iota((1024, 128), 1)
    place = jnp.bitwise_and(iota((1024, 128), 0), 31)
    first = jnp.zeros((1024, 128), F32)
    for q in range(2):
        column = jnp.broadcast_to(pixels[pl.ds(2048 + q, 1024, stride=2), :][:, :1], (1024, 128))
        first = jnp.where(lane == place + 32 * q, column, first)
    by_owner = jnp.where(
        lax.shift_right_logical(iota((NT * 16, 1024), 1), 5) * 16 == iota((NT * 16, 1024), 0), 1.0, 0.0
    ).astype(BF)
    lone = dot(by_owner, first.astype(BF)).astype(BF)
    past = iota((64, 128), 1) > 0
    for t in range(NT):
        out[t * ROWS : t * ROWS + 64, :] = (
            pixels[t * 64 : t * 64 + 64, :]
            + jnp.where(past, pixels[2048 + t * 64 : 2048 + t * 64 + 64, :], 0.0)
        ).astype(BF)
        out[t * ROWS + 64 : t * ROWS + ROWS, :] = lone[t * 16 : t * 16 + 16]


def grid_and_rows(facts, recv, table, weight, over_r, over_x):
    vmem = pl.BlockSpec(memory_space=pltpu.VMEM)
    return pl.pallas_call(
        grid_body,
        out_shape=jax.ShapeDtypeStruct((NT * ROWS, 128), BF),
        in_specs=[pl.BlockSpec(memory_space=pltpu.SMEM)] + [vmem] * 5,
        out_specs=vmem,
        scratch_shapes=[
            pltpu.VMEM((512 * GS, 128), F32),
            pltpu.VMEM((2 * 128 * HS, 128), F32),
            pltpu.VMEM((ALL, 128), F32),
            pltpu.VMEM((ALL, 128), F32),
            pltpu.SMEM((ALL + 64,), jnp.int32),
        ],
        compiler_params=pltpu.CompilerParams(vmem_limit_bytes=56 * MIB),
        name="grid_and_rows",
    )(facts, recv, table, weight, over_r, over_x)


def finish_body(first, pixels, facts, over_t, lone_t, over_j_hbm, *rest):
    if first:
        out, most, *rest, mine, seen, send_y, recv_y = rest
    else:
        out, *rest = rest
    recv, wide, middle, lone, fold, last, over_j, send_a, recv_a, send_b, recv_b, table_sem = rest
    fetch = pltpu.make_async_copy(over_j_hbm, over_j, table_sem)
    fetch.start()
    me = lax.axis_index("tile")
    chan = lax.axis_index("chan")
    home = me // 8
    stays = home == chan
    barrier = pltpu.get_barrier_semaphore()

    def greet(i, _):
        pl.semaphore_signal(
            barrier, inc=1, device_id=(lax.rem(me + i, NT), chan), device_id_type=MESH
        )
        return 0

    lax.fori_loop(1, NT, greet, 0)

    def greet_source(i, _):
        from_t, from_c = chan * 8 + i // NC, lax.rem(i, NC)

        @pl.when(jnp.logical_or(from_t != me, from_c != chan))
        def _():
            pl.semaphore_signal(barrier, inc=1, device_id=(from_t, from_c), device_id_type=MESH)

        return 0

    lax.fori_loop(0, NT, greet_source, 0)
    greeted = 2 * NT - 1
    if first:
        greeted += NC - 1
        for i in range(1, NC):
            pl.semaphore_signal(
                barrier, inc=1, device_id=(me, lax.rem(chan + i, NC)), device_id_type=MESH
            )
    pl.semaphore_wait(barrier, jnp.where(stays, greeted - 1, greeted))

    def copy(i):
        to = lax.rem(me + i, NT)
        return pltpu.make_async_remote_copy(
            src_ref=pixels.at[pl.ds(pl.multiple_of(to * ROWS, 16), ROWS)],
            dst_ref=recv.at[pl.ds(pl.multiple_of(me * ROWS, 16), ROWS)],
            send_sem=send_a.at[i],
            recv_sem=recv_a.at[i],
            device_id=(to, chan),
            device_id_type=MESH,
        )

    def start(i, _):
        copy(i).start()
        return 0

    lax.fori_loop(1, NT, start, 0)
    if first:
        known = jnp.where(iota((NT, 128), 1) < 112, 0, facts[...]).astype(F32)
        known = jnp.max(jnp.max(known, axis=0, keepdims=True), axis=1, keepdims=True)
        mine[...] = jnp.broadcast_to(known, (8, 128))

        def tell(i):
            return pltpu.make_async_remote_copy(
                src_ref=mine,
                dst_ref=seen.at[i],
                send_sem=send_y.at[i],
                recv_sem=recv_y.at[i],
                device_id=(me, lax.rem(chan + i, NC)),
                device_id_type=MESH,
            )

        for i in range(1, NC):
            tell(i).start()
    own = pl.ds(pl.multiple_of(me * ROWS, 16), ROWS)
    recv[own, :] = pixels[own, :]

    def wait(i, _):
        copy(i).wait()
        return 0

    lax.fori_loop(1, NT, wait, 0)

    def widen(t, _):
        block = recv[pl.ds(pl.multiple_of(t * ROWS, 16), ROWS), :].astype(F32)
        wide[pl.ds(t * WS, 64), :] = block[:64]
        lone[pl.ds(t, 1), :] = block[64:65]
        return 0

    lax.fori_loop(0, NT, widen, 0, unroll=4)

    def over_tiles(l, _):
        rows = [wide[pl.ds(2 * l + q, NT, stride=WS), :] for q in range(2)]
        got = dot(over_t[...], jnp.concatenate(rows, axis=0).astype(BF))
        middle[pl.ds(l * MS, 128), :] = got[:128] + got[128:]
        return 0

    lax.fori_loop(0, 32, over_tiles, 0, unroll=8)
    fetch.wait()
    alone = dot(lone_t[...], lone[...].astype(BF))
    wide[0:64, :] = alone[:64] - pltpu.roll(alone[64:], 96, 1)

    def over_columns(a, _):
        for h in range(2):
            made = []
            for b in range(4):
                m0 = h * 32 + b * 8 + a
                right = jnp.concatenate(
                    [middle[pl.ds(64 * q + m0, 32, stride=MS), :] for q in range(2)], axis=1
                )
                high = right.astype(BF)
                low = (right - high.astype(F32)).astype(BF)
                left = over_j[pl.ds(pl.multiple_of(m0 * 32, 32), 32), :]
                got = dot_t(left, high)
                got = got[:16] + got[16:] + dot_t(left[:16], low)
                made.append(got + wide[pl.ds(m0, 1), :][:, :32])
            fold[pl.ds(h * 8 + a, 16, stride=16), :] = jnp.concatenate(made, axis=1)
        return 0

    lax.fori_loop(0, 8, over_columns, 0, unroll=2)
    slot = lax.rem(me, 8) * NC + chan

    def give(i):
        to = lax.rem(me + i, NT)
        return pltpu.make_async_remote_copy(
            src_ref=fold.at[pl.ds(pl.multiple_of(to * 8, 8), 8)],
            dst_ref=last.at[pl.ds(pl.multiple_of(slot * 8, 8), 8)],
            send_sem=send_b.at[i],
            recv_sem=recv_b.at[slot],
            device_id=(to, home),
            device_id_type=MESH,
        )

    def take(i):
        at = pl.ds(pl.multiple_of(i * 8, 8), 8)
        return pltpu.make_async_remote_copy(
            src_ref=last.at[at],
            dst_ref=last.at[at],
            send_sem=send_b.at[i],
            recv_sem=recv_b.at[i],
            device_id=(chan * 8 + i // NC, lax.rem(i, NC)),
            device_id_type=MESH,
        )

    @pl.when(jnp.logical_not(stays))
    def _():
        give(0).start()

    @pl.when(stays)
    def _():
        last[pl.ds(pl.multiple_of(slot * 8, 8), 8), :] = fold[
            pl.ds(pl.multiple_of(me * 8, 8), 8), :
        ]

    def start_b(i, _):
        give(i).start()
        return 0

    lax.fori_loop(1, NT, start_b, 0)
    if first:
        for i in range(1, NC):
            tell(i).wait()
            known = jnp.maximum(known, jnp.max(seen[i][:1], axis=1, keepdims=True))
        most[0, 0] = jnp.max(known)

    def wait_b(i, _):
        @pl.when(jnp.logical_or(jnp.logical_not(stays), i != slot))
        def _():
            take(i).wait_recv()

        return 0

    lax.fori_loop(0, NT, wait_b, 0)
    for t in range(8):
        total = last[t * 32 : t * 32 + 8, :]
        for c in range(1, NC):
            total = total + last[t * 32 + c * 8 : t * 32 + c * 8 + 8, :]
        out[t * 8 : t * 8 + 8, :] = total

    @pl.when(jnp.logical_not(stays))
    def _():
        give(0).wait_send()

    def sent_b(i, _):
        give(i).wait_send()
        return 0

    lax.fori_loop(1, NT, sent_b, 0)


def finish(first, pixels, facts, over_t, lone_t, over_j):
    vmem = pl.BlockSpec(memory_space=pltpu.VMEM)
    shapes, outs = [jax.ShapeDtypeStruct((64, 128), F32)], [vmem]
    scratch = [
        pltpu.VMEM((NT * ROWS, 128), BF),
        pltpu.VMEM((NT * WS, 128), F32),
        pltpu.VMEM((32 * MS, 128), F32),
        pltpu.VMEM((NT, 128), F32),
        pltpu.VMEM((256, 128), F32),
        pltpu.VMEM((256, 128), F32),
        pltpu.VMEM((2048, 256), BF),
        pltpu.SemaphoreType.DMA((NT,)),
        pltpu.SemaphoreType.DMA((NT,)),
        pltpu.SemaphoreType.DMA((NT,)),
        pltpu.SemaphoreType.DMA((NT,)),
        pltpu.SemaphoreType.DMA,
    ]
    if first:
        shapes.append(jax.ShapeDtypeStruct((1, 1), F32))
        outs.append(pl.BlockSpec(memory_space=pltpu.SMEM))
        scratch += [
            pltpu.VMEM((8, 128), F32),
            pltpu.VMEM((NC, 8, 128), F32),
            pltpu.SemaphoreType.DMA((NC,)),
            pltpu.SemaphoreType.DMA((NC,)),
        ]
    return pl.pallas_call(
        functools.partial(finish_body, first),
        out_shape=shapes,
        in_specs=[vmem] * 4 + [pl.BlockSpec(memory_space=pltpu.HBM)],
        out_specs=outs,
        scratch_shapes=scratch,
        compiler_params=pltpu.CompilerParams(
            collective_id=1 if first else 3, has_side_effects=True, vmem_limit_bytes=60 * MIB
        ),
        name="finish" if first else "finish_more",
    )(pixels, facts, over_t, lone_t, over_j)


def local(visibilities, kernels, destination, cell, plane):
    over_r, over_x = (jnp.asarray(t) for t in row_tables())
    over_t, over_j, lone_t = (jnp.asarray(t) for t in column_tables())
    samples = visibilities[0]
    dest = destination.reshape(1, BLK)
    kern = kernels.reshape(NW * 128, 128)
    none = jnp.zeros((1, BLK), jnp.int32)
    recv, facts, table, weight = exchange(True, samples, dest, cell, plane, none, kern)
    pixels = grid_and_rows(facts, recv, table, weight, over_r, over_x)
    image, most = finish(True, pixels, facts, over_t, lone_t, over_j)
    most = most[0, 0]

    def more(image):
        def again(state):
            done, total = state
            skipped = jnp.broadcast_to(done, (1, BLK))
            recv, facts = exchange(False, samples, dest, cell, plane, skipped)
            pixels = grid_and_rows(facts, recv, table, weight, over_r, over_x)
            [terms] = finish(False, pixels, facts, over_t, lone_t, over_j)
            return done + CAP, total + terms

        return lax.while_loop(
            lambda state: state[0].astype(F32) < most, again, (jnp.int32(CAP), image)
        )[1]

    image = lax.cond(most > CAP, more, lambda terms: terms, image)
    return image.reshape(8, 8, 4, 32).transpose(0, 3, 2, 1).reshape(256, 32)


def solution(mesh):
    placed = (
        P("chan", "tile", None),
        P("chan", None, None, None, None),
        P("chan", "tile", None),
        P("chan", "tile"),
        P("chan", "tile"),
    )
    return jax.shard_map(
        local, mesh=mesh, in_specs=placed, out_specs=P("chan", "tile"), check_vma=False
    )
```

```python
import functools
import math

import jax
import jax.numpy as jnp
import ml_dtypes
import numpy as np
from jax import lax
from jax.experimental import pallas as pl
from jax.experimental.pallas import tpu as pltpu
from jax.sharding import PartitionSpec as P

G = 8192
S = 64
NW = 32
PIX = 1024
NT = 32
NC = 4
BLK = 256
CAP = 31
GS = 65
HS = 129
TOGETHER = 32
WS = 65
MS = 129
ROWS = 80
SLOTS = 32
ALL = NT * SLOTS
MIB = 1 << 20
BF = jnp.bfloat16
F32 = jnp.float32
MESH = pl.DeviceIdType.MESH
HALF = jax.ShapeDtypeStruct((2 * 128 * HS, 128), F32)


def split(table):
    high = table.astype(np.float32).astype(ml_dtypes.bfloat16)
    low = (table - high.astype(np.float64)).astype(ml_dtypes.bfloat16)
    return high, low


def row_tables():
    step = G // PIX - 1
    l0 = np.arange(128)
    angle = 2 * math.pi / 128 * ((step * (l0[:, None] - PIX // 2) * (l0[None, :] - 64)) % 128)
    c, s = np.cos(angle), np.sin(angle)
    over_r = np.block([[c, -s], [s, c]]).astype(np.float32).astype(ml_dtypes.bfloat16)
    pixel = l0[:, None] + 128 * np.arange(8)[None, :]
    angle = 2 * math.pi / G * ((step * (pixel[:, :, None] - PIX // 2) * np.arange(S)) % G)
    c, s = np.cos(angle), np.sin(angle)
    over_x = np.concatenate([np.concatenate([c, -s], 2), np.concatenate([s, c], 2)], 1)
    high, low = split(over_x)
    return over_r, np.concatenate([high, low], 1).reshape(128 * 32, 128)


def column_tables():
    step = G // PIX - 1
    m0 = np.arange(64)
    tile = np.arange(NT)
    angle = 2 * math.pi / 64 * ((step * (m0[:, None] - PIX // 2) * (tile[None, :] - NT)) % 64)
    c, s = np.cos(angle), np.sin(angle)
    over_t = np.concatenate(split(np.block([[c, -s], [s, c]])), 0)
    pixel = m0[:, None] + 64 * np.arange(16)[None, :]
    angle = 2 * math.pi / G * ((step * (pixel[:, :, None] - PIX // 2) * np.arange(128)) % G)
    over_j = np.concatenate([np.cos(angle), -np.sin(angle)], 2) / G
    high, low = split(over_j)
    angle = 2 * math.pi / 64 * ((step * (m0[:, None] - PIX // 2) * (tile[None, :] + 1 - NT)) % 64)
    lone = np.concatenate([np.cos(angle), np.sin(angle)], 0) / G
    return over_t, np.concatenate([high, low], 1).reshape(64 * 32, 256), split(lone)[0]


def iota(shape, axis):
    return lax.broadcasted_iota(jnp.int32, shape, axis)


def dot(a, b):
    return jnp.dot(a, b, preferred_element_type=F32)


def dot_t(a, b):
    return lax.dot_general(a, b, (((1,), (1,)), ((), ())), preferred_element_type=F32)


def fill_slots(samples, dest, cell, plane, skipped):
    column = jnp.bitwise_and(cell, 127)
    mirror = lax.shift_right_logical(column, 6)
    column = jnp.where(mirror == 1, 127 - column, column)
    owner = lax.shift_right_logical(column, 1)
    inner = jnp.bitwise_and(column, 1) + 2 * mirror
    row = dest * 4 + lax.shift_right_logical(cell, 7)
    named = iota((NT, BLK), 0) == owner
    one = jnp.where(named, 1.0, 0.0)
    one_b = one.astype(BF)
    before = jnp.where(iota((BLK, BLK), 0) < iota((BLK, BLK), 1), 1.0, 0.0).astype(BF)
    count = dot(one_b, before)
    rank = jnp.sum(one * count, axis=0, keepdims=True).astype(jnp.int32) - skipped
    here = jnp.logical_and(rank >= 0, rank < CAP)
    slot = jnp.where(here, owner * SLOTS + rank, -1)
    pick = jnp.where(iota((ALL, BLK), 0) == slot, 1.0, 0.0).astype(BF)
    lane = iota((128, BLK), 0)
    kind = lax.shift_right_logical(lane, 5)
    value = jnp.where(kind == 0, row, jnp.where(kind == 1, plane, jnp.where(kind == 2, inner, 1)))
    held = jnp.logical_and(here, jnp.logical_or(kind == 3, jnp.bitwise_and(lane, 31) == rank))
    facts = dot_t(one_b, jnp.where(held, value.astype(F32), 0.0).astype(BF))
    named_most = jnp.max(jnp.sum(one, axis=1, keepdims=True), axis=0, keepdims=True)
    facts = jnp.where(iota((NT, 128), 1) < 112, facts, named_most)
    last = jnp.where(iota((ALL, NT), 0) == iota((ALL, NT), 1) * SLOTS + CAP, 1.0, 0.0).astype(BF)
    slots = dot(pick, samples.astype(BF)) + dot(last, facts.astype(BF))
    return slots.astype(BF)


def exchange_body(first, samples, dest, cell, plane, *rest):
    if first:
        kern_hbm, recv, facts, table, weight, send, send_sem, recv_sem, kern, kern_sem = rest
    else:
        skipped, recv, facts, send, send_sem, recv_sem = rest
    me = lax.axis_index("tile")
    chan = lax.axis_index("chan")
    barrier = pltpu.get_barrier_semaphore()
    fetch = pltpu.make_async_copy(kern_hbm, kern, kern_sem) if first else None
    if first:
        fetch.start()

    def greet(i, _):
        pl.semaphore_signal(
            barrier, inc=1, device_id=(lax.rem(me + i, NT), chan), device_id_type=MESH
        )
        return 0

    lax.fori_loop(1, NT, greet, 0)
    send[...] = fill_slots(samples[...], dest[...], cell[...], plane[...], 0 if first else skipped[...])
    pl.semaphore_wait(barrier, NT - 1)

    def copy(i):
        to = lax.rem(me + i, NT)
        return pltpu.make_async_remote_copy(
            src_ref=send.at[pl.ds(pl.multiple_of(to * SLOTS, SLOTS), SLOTS)],
            dst_ref=recv.at[pl.ds(pl.multiple_of(me * SLOTS, SLOTS), SLOTS)],
            send_sem=send_sem.at[i],
            recv_sem=recv_sem.at[i],
            device_id=(to, chan),
            device_id_type=MESH,
        )

    def start(i, _):
        copy(i).start()
        return 0

    lax.fori_loop(1, NT, start, 0)
    own = pl.ds(pl.multiple_of(me * SLOTS, SLOTS), SLOTS)
    recv[own, :] = send[own, :]
    if first:
        low = iota((S, 128), 1) < S
        mirrored = jnp.where(iota((128, 128), 0) + iota((128, 128), 1) == 191, 1.0, 0.0).astype(BF)

        def prepare(w, _):
            base = pl.multiple_of(w * 128, 128)
            both = kern[pl.ds(base, 128), :].astype(F32)
            real, imag = both[:S], both[S:]
            turned = both.T[:S]
            table[pl.ds(base, S), :] = turned
            swapped = pltpu.roll(turned, S, 1)
            table[pl.ds(base + S, S), :] = jnp.where(low, -swapped, swapped)
            for side in range(2):
                at = base + side * NW * 128
                weight[pl.ds(at, S), :] = jnp.where(low, pltpu.roll(real, S, 1), imag).astype(BF)
                weight[pl.ds(at + S, S), :] = jnp.where(
                    low, -pltpu.roll(imag, S, 1), real
                ).astype(BF)
                if side == 0:
                    both = dot(kern[pl.ds(base, 128), :], mirrored)
                    real, imag = both[:S], both[S:]
            return 0

        fetch.wait()
        lax.fori_loop(0, NW, prepare, 0, unroll=2)

    def wait(i, _):
        copy(i).wait()
        return 0

    lax.fori_loop(1, NT, wait, 0)
    last = jnp.where(iota((NT, ALL), 1) == iota((NT, ALL), 0) * SLOTS + CAP, 1.0, 0.0).astype(BF)
    raw = dot(last, recv[...])
    lane = iota((NT, 128), 1)
    code = (pltpu.roll(raw, 64, 1) * 128.0 + raw) * 32.0 + pltpu.roll(raw, 96, 1)
    facts[...] = jnp.where(lane < SLOTS, code, raw).astype(jnp.int32)


def exchange(first, samples, dest, cell, plane, last):
    vmem = pl.BlockSpec(memory_space=pltpu.VMEM)
    shapes = [jax.ShapeDtypeStruct((ALL, 128), BF), jax.ShapeDtypeStruct((NT, 128), jnp.int32)]
    operands = [samples, dest, cell, plane, last]
    specs = [vmem] * 4 + [pl.BlockSpec(memory_space=pltpu.HBM) if first else vmem]
    scratch = [
        pltpu.VMEM((ALL, 128), BF),
        pltpu.SemaphoreType.DMA((NT,)),
        pltpu.SemaphoreType.DMA((NT,)),
    ]
    if first:
        shapes += [
            jax.ShapeDtypeStruct((NW * 128, 128), F32),
            jax.ShapeDtypeStruct((2 * NW * 128, 128), BF),
        ]
        scratch += [
            pltpu.VMEM((NW * 128, 128), BF),
            pltpu.SemaphoreType.DMA,
        ]
    return pl.pallas_call(
        functools.partial(exchange_body, first),
        out_shape=shapes,
        in_specs=specs,
        out_specs=[vmem] * len(shapes),
        scratch_shapes=scratch,
        compiler_params=pltpu.CompilerParams(
            collective_id=0 if first else 2, has_side_effects=True, vmem_limit_bytes=40 * MIB
        ),
        name="exchange" if first else "exchange_more",
    )(*operands)


def grid_body(facts, recv, table, weight, over_r, half, grid, fill_a, fill_b, todo):
    lane = iota((ALL, 128), 1)
    slot = iota((ALL, 128), 0)
    blocks = jnp.where(jnp.bitwise_and(slot, SLOTS - 1) == CAP, 0.0, recv[...].astype(F32))
    swapped = pltpu.roll(blocks, S, 1)
    fill_a[...] = jnp.where(lane < S, blocks, swapped)
    fill_b[...] = jnp.where(lane < S, swapped, blocks)

    def from_source(t, at):
        part = grid.shape[0] // NT
        grid[pl.ds(pl.multiple_of(t * part, 8), part), :] = jnp.zeros((part, 128), F32)
        for i in range(SLOTS):
            todo[at + i] = facts[t, i] * ALL + t * SLOTS + i
        return at + facts[t, 96]

    number = lax.fori_loop(0, NT, from_source, 0)
    for k in range(TOGETHER):
        todo[number + k] = CAP

    def blocks_together(j, _):
        made = []
        for k in range(TOGETHER):
            code = todo[j * TOGETHER + k]
            i = jnp.bitwise_and(code, ALL - 1)
            fact = lax.shift_right_logical(code, 10)
            base = pl.multiple_of(jnp.bitwise_and(fact, 31) * 128, 128)
            left = (
                fill_a[pl.ds(i, 1), :] * table[pl.ds(base, S), :]
                + fill_b[pl.ds(i, 1), :] * table[pl.ds(base + S, S), :]
            ).astype(BF)
            side = lax.shift_right_logical(fact, 13)
            patch = dot(left, weight[pl.ds(pl.multiple_of(base + side * NW * 128, 128), 128), :])
            made.append((lax.shift_right_logical(fact, 5), patch))
        for place, patch in made:
            at = pl.ds(place * GS, S)
            grid[at, :] = grid[at, :] + patch
        return 0

    lax.fori_loop(0, (number + TOGETHER - 1) // TOGETHER, blocks_together, 0)

    def over_rows(x, _):
        part = [grid[pl.ds(i * 128 * GS + x, 128, stride=GS), :] for i in range(4)]
        real = jnp.concatenate([p[:, :S] for p in part], axis=1)
        imag = jnp.concatenate([p[:, S:] for p in part], axis=1)
        got = dot(over_r[...], jnp.concatenate([real, imag], axis=0).astype(BF))
        half[pl.ds(x, 128, stride=HS), :] = got[:128, :128]
        half[pl.ds(S + x, 128, stride=HS), :] = got[128:, :128]
        half[pl.ds(128 * HS + x, 128, stride=HS), :] = got[:128, 128:]
        half[pl.ds(128 * HS + S + x, 128, stride=HS), :] = got[128:, 128:]
        return 0

    lax.fori_loop(0, S, over_rows, 0, unroll=8)


def grid_and_rows(facts, recv, table, weight, over_r):
    vmem = pl.BlockSpec(memory_space=pltpu.VMEM)
    return pl.pallas_call(
        grid_body,
        out_shape=HALF,
        in_specs=[pl.BlockSpec(memory_space=pltpu.SMEM)] + [vmem] * 4,
        out_specs=vmem,
        scratch_shapes=[
            pltpu.VMEM((512 * GS, 128), F32),
            pltpu.VMEM((ALL, 128), F32),
            pltpu.VMEM((ALL, 128), F32),
            pltpu.SMEM((ALL + 64,), jnp.int32),
        ],
        compiler_params=pltpu.CompilerParams(vmem_limit_bytes=24 * MIB),
        name="grid_and_rows",
    )(facts, recv, table, weight, over_r)


def finish_body(first, half, facts, over_x, over_t, lone_t, over_j, *rest):
    if first:
        out, most, *rest, mine, seen, send_y, recv_y = rest
    else:
        out, *rest = rest
    pixels, send, recv, wide, middle, lone, fold, last, send_a, recv_a, send_b, recv_b = rest
    me = lax.axis_index("tile")
    chan = lax.axis_index("chan")
    home = me // 8
    stays = home == chan
    barrier = pltpu.get_barrier_semaphore()

    def greet(i, _):
        pl.semaphore_signal(
            barrier, inc=1, device_id=(lax.rem(me + i, NT), chan), device_id_type=MESH
        )
        return 0

    lax.fori_loop(1, NT, greet, 0)

    def greet_source(i, _):
        from_t, from_c = chan * 8 + i // NC, lax.rem(i, NC)

        @pl.when(jnp.logical_or(from_t != me, from_c != chan))
        def _():
            pl.semaphore_signal(barrier, inc=1, device_id=(from_t, from_c), device_id_type=MESH)

        return 0

    lax.fori_loop(0, NT, greet_source, 0)
    greeted = 2 * NT - 1
    if first:
        greeted += NC - 1
        for i in range(1, NC):
            pl.semaphore_signal(
                barrier, inc=1, device_id=(me, lax.rem(chan + i, NC)), device_id_type=MESH
            )

    def give_rows(to):
        return pltpu.make_async_remote_copy(
            src_ref=send.at[pl.ds(pl.multiple_of(to * ROWS, 16), ROWS)],
            dst_ref=recv.at[pl.ds(pl.multiple_of(me * ROWS, 16), ROWS)],
            send_sem=send_a.at[to],
            recv_sem=recv_a.at[me],
            device_id=(to, chan),
            device_id_type=MESH,
        )

    def take_rows(source):
        at = pl.ds(pl.multiple_of(source * ROWS, 16), ROWS)
        return pltpu.make_async_remote_copy(
            src_ref=recv.at[at],
            dst_ref=recv.at[at],
            send_sem=send_a.at[source],
            recv_sem=recv_a.at[source],
            device_id=(source, chan),
            device_id_type=MESH,
        )

    def over_offsets(l0):
        at = l0 * HS
        right = jnp.concatenate(
            [half[pl.ds(at, 128), :], half[pl.ds(128 * HS + at, 128), :]], axis=1
        ).astype(BF)
        got = dot(over_x[pl.ds(pl.multiple_of(l0 * 32, 32), 32), :], right)
        got = got[:16] + got[16:]
        turned = pltpu.roll(got[:, 128:], 1, 1)
        for q in range(2):
            rows = slice(8 * q, 8 * q + 8)
            pixels[pl.ds(2 * l0 + q, 8, stride=256), :] = got[rows, :128]
            pixels[pl.ds(2048 + 2 * l0 + q, 8, stride=256), :] = (
                turned[rows] if q == 0 else -turned[rows]
            )

    past = iota((64, 128), 1) > 0
    lane = iota((32, 128), 1)
    place = iota((32, 128), 0)

    def pack(i, part):
        to = jnp.bitwise_and(i + me // 4, 7) * 4 + part
        rows = pl.multiple_of(to * 64, 64)
        mirror = pixels[pl.ds(2048 + rows, 64), :]
        at = pl.multiple_of(to * ROWS, 16)
        send[pl.ds(at, 64), :] = (
            pixels[pl.ds(rows, 64), :] + jnp.where(past, mirror, 0.0)
        ).astype(BF)
        spread = jnp.zeros((32, 128), F32)
        for q in range(2):
            column = pixels[pl.ds(2048 + rows + q, 32, stride=2), :][:, :1]
            spread = jnp.where(
                lane == place + 32 * q, jnp.broadcast_to(column, (32, 128)), spread
            )
        spread = jnp.sum(spread, axis=0, keepdims=True)
        send[pl.ds(at + 64, 16), :] = jnp.broadcast_to(spread, (16, 128)).astype(BF)
        return part

    def start(i, part):
        to = jnp.bitwise_and(i + me // 4, 7) * 4 + part

        @pl.when(to != me)
        def _():
            give_rows(to).start()

        return part

    for turn in range(4):
        part = jnp.bitwise_and(me + turn, 3)

        def some(j, part):
            for k in range(16):
                over_offsets(part * 32 + j * 16 + k)
            return part

        lax.fori_loop(0, 2, some, part)
        lax.fori_loop(0, 8, pack, part, unroll=2)
        if turn == 0:
            pl.semaphore_wait(barrier, jnp.where(stays, greeted - 1, greeted))
        lax.fori_loop(0, 8, start, part)
    if first:
        known = jnp.where(iota((NT, 128), 1) < 112, 0, facts[...]).astype(F32)
        known = jnp.max(jnp.max(known, axis=0, keepdims=True), axis=1, keepdims=True)
        mine[...] = jnp.broadcast_to(known, (8, 128))

        def tell(i):
            return pltpu.make_async_remote_copy(
                src_ref=mine,
                dst_ref=seen.at[i],
                send_sem=send_y.at[i],
                recv_sem=recv_y.at[i],
                device_id=(me, lax.rem(chan + i, NC)),
                device_id_type=MESH,
            )

        for i in range(1, NC):
            tell(i).start()
    own = pl.ds(pl.multiple_of(me * ROWS, 16), ROWS)
    recv[own, :] = send[own, :]

    def wait(i, _):
        take_rows(lax.rem(me + i, NT)).wait_recv()
        return 0

    lax.fori_loop(1, NT, wait, 0)

    def widen(t, _):
        block = recv[pl.ds(pl.multiple_of(t * ROWS, 16), ROWS), :].astype(F32)
        wide[pl.ds(t * WS, 64), :] = block[:64]
        lone[pl.ds(t, 1), :] = block[64:65]
        return 0

    lax.fori_loop(0, NT, widen, 0, unroll=4)

    def over_tiles(l, _):
        rows = [wide[pl.ds(2 * l + q, NT, stride=WS), :] for q in range(2)]
        got = dot(over_t[...], jnp.concatenate(rows, axis=0).astype(BF))
        middle[pl.ds(l * MS, 128), :] = got[:128] + got[128:]
        return 0

    lax.fori_loop(0, 32, over_tiles, 0, unroll=8)
    alone = dot(lone_t[...], lone[...].astype(BF))
    wide[0:64, :] = alone[:64] - pltpu.roll(alone[64:], 96, 1)

    def over_columns(a, _):
        for h in range(2):
            made = []
            for b in range(4):
                m0 = h * 32 + b * 8 + a
                right = jnp.concatenate(
                    [middle[pl.ds(64 * q + m0, 32, stride=MS), :] for q in range(2)], axis=1
                )
                high = right.astype(BF)
                low = (right - high.astype(F32)).astype(BF)
                left = over_j[pl.ds(pl.multiple_of(m0 * 32, 32), 32), :]
                got = dot_t(left, high)
                got = got[:16] + got[16:] + dot_t(left[:16], low)
                made.append(got + wide[pl.ds(m0, 1), :][:, :32])
            fold[pl.ds(h * 8 + a, 16, stride=16), :] = jnp.concatenate(made, axis=1)
        return 0

    lax.fori_loop(0, 8, over_columns, 0, unroll=2)
    slot = lax.rem(me, 8) * NC + chan

    def give(i):
        to = lax.rem(me + i, NT)
        return pltpu.make_async_remote_copy(
            src_ref=fold.at[pl.ds(pl.multiple_of(to * 8, 8), 8)],
            dst_ref=last.at[pl.ds(pl.multiple_of(slot * 8, 8), 8)],
            send_sem=send_b.at[i],
            recv_sem=recv_b.at[slot],
            device_id=(to, home),
            device_id_type=MESH,
        )

    def take(i):
        at = pl.ds(pl.multiple_of(i * 8, 8), 8)
        return pltpu.make_async_remote_copy(
            src_ref=last.at[at],
            dst_ref=last.at[at],
            send_sem=send_b.at[i],
            recv_sem=recv_b.at[i],
            device_id=(chan * 8 + i // NC, lax.rem(i, NC)),
            device_id_type=MESH,
        )

    @pl.when(jnp.logical_not(stays))
    def _():
        give(0).start()

    @pl.when(stays)
    def _():
        last[pl.ds(pl.multiple_of(slot * 8, 8), 8), :] = fold[
            pl.ds(pl.multiple_of(me * 8, 8), 8), :
        ]

    def start_b(i, _):
        give(i).start()
        return 0

    lax.fori_loop(1, NT, start_b, 0)
    if first:
        for i in range(1, NC):
            tell(i).wait()
            known = jnp.maximum(known, jnp.max(seen[i][:1], axis=1, keepdims=True))
        most[0, 0] = jnp.max(known)

    def wait_b(i, _):
        @pl.when(jnp.logical_or(jnp.logical_not(stays), i != slot))
        def _():
            take(i).wait_recv()

        return 0

    lax.fori_loop(0, NT, wait_b, 0)
    for t in range(8):
        total = last[t * 32 : t * 32 + 8, :]
        for c in range(1, NC):
            total = total + last[t * 32 + c * 8 : t * 32 + c * 8 + 8, :]
        out[t * 8 : t * 8 + 8, :] = total

    @pl.when(jnp.logical_not(stays))
    def _():
        give(0).wait_send()

    def sent_b(i, _):
        give(i).wait_send()
        return 0

    lax.fori_loop(1, NT, sent_b, 0)

    def sent_a(i, _):
        give_rows(lax.rem(me + i, NT)).wait_send()
        return 0

    lax.fori_loop(1, NT, sent_a, 0)


def finish(first, half, facts, over_x, over_t, lone_t, over_j):
    vmem = pl.BlockSpec(memory_space=pltpu.VMEM)
    shapes, outs = [jax.ShapeDtypeStruct((64, 128), F32)], [vmem]
    scratch = [
        pltpu.VMEM((4096, 128), F32),
        pltpu.VMEM((NT * ROWS, 128), BF),
        pltpu.VMEM((NT * ROWS, 128), BF),
        pltpu.VMEM((NT * WS, 128), F32),
        pltpu.VMEM((32 * MS, 128), F32),
        pltpu.VMEM((NT, 128), F32),
        pltpu.VMEM((256, 128), F32),
        pltpu.VMEM((256, 128), F32),
        pltpu.SemaphoreType.DMA((NT,)),
        pltpu.SemaphoreType.DMA((NT,)),
        pltpu.SemaphoreType.DMA((NT,)),
        pltpu.SemaphoreType.DMA((NT,)),
    ]
    if first:
        shapes.append(jax.ShapeDtypeStruct((1, 1), F32))
        outs.append(pl.BlockSpec(memory_space=pltpu.SMEM))
        scratch += [
            pltpu.VMEM((8, 128), F32),
            pltpu.VMEM((NC, 8, 128), F32),
            pltpu.SemaphoreType.DMA((NC,)),
            pltpu.SemaphoreType.DMA((NC,)),
        ]
    return pl.pallas_call(
        functools.partial(finish_body, first),
        out_shape=shapes,
        in_specs=[vmem] * 6,
        out_specs=outs,
        scratch_shapes=scratch,
        compiler_params=pltpu.CompilerParams(
            collective_id=1 if first else 3, has_side_effects=True, vmem_limit_bytes=20 * MIB
        ),
        name="finish" if first else "finish_more",
    )(half, facts, over_x, over_t, lone_t, over_j)


def local(visibilities, kernels, destination, cell, plane):
    over_r, over_x = (jnp.asarray(t) for t in row_tables())
    over_t, over_j, lone_t = (jnp.asarray(t) for t in column_tables())
    samples = visibilities[0]
    dest = destination.reshape(1, BLK)
    kern = kernels.reshape(NW * 128, 128)
    recv, facts, table, weight = exchange(True, samples, dest, cell, plane, kern)
    half = grid_and_rows(facts, recv, table, weight, over_r)
    image, most = finish(True, half, facts, over_x, over_t, lone_t, over_j)
    most = most[0, 0]

    def more(image):
        def again(state):
            done, total = state
            skipped = jnp.broadcast_to(done, (1, BLK))
            recv, facts = exchange(False, samples, dest, cell, plane, skipped)
            half = grid_and_rows(facts, recv, table, weight, over_r)
            [terms] = finish(False, half, facts, over_x, over_t, lone_t, over_j)
            return done + CAP, total + terms

        return lax.while_loop(
            lambda state: state[0].astype(F32) < most, again, (jnp.int32(CAP), image)
        )[1]

    image = lax.cond(most > CAP, more, lambda terms: terms, image)
    return image.reshape(8, 8, 4, 32).transpose(0, 3, 2, 1).reshape(256, 32)


def solution(mesh):
    placed = (
        P("chan", "tile", None),
        P("chan", None, None, None, None),
        P("chan", "tile", None),
        P("chan", "tile"),
        P("chan", "tile"),
    )
    return jax.shard_map(
        local, mesh=mesh, in_specs=placed, out_specs=P("chan", "tile"), check_vma=False
    )
```

```python
import functools
import math

import jax
import jax.numpy as jnp
import ml_dtypes
import numpy as np
from jax import lax
from jax.experimental import pallas as pl
from jax.experimental.pallas import tpu as pltpu
from jax.sharding import PartitionSpec as P

G = 8192
S = 64
NW = 32
PIX = 1024
NT = 32
NC = 4
BLK = 256
CAP = 31
GS = 65
HS = 129
TOGETHER = 48
WS = 65
MS = 129
SLOTS = 32
ALL = NT * SLOTS
MIB = 1 << 20
BF = jnp.bfloat16
F32 = jnp.float32
MESH = pl.DeviceIdType.MESH


def split(table):
    high = table.astype(np.float32).astype(ml_dtypes.bfloat16)
    low = (table - high.astype(np.float64)).astype(ml_dtypes.bfloat16)
    return high, low


def row_tables():
    step = G // PIX - 1
    l0 = np.arange(128)
    angle = 2 * math.pi / 128 * ((step * (l0[:, None] - PIX // 2) * (l0[None, :] - 64)) % 128)
    c, s = np.cos(angle), np.sin(angle)
    over_r = np.block([[c, -s], [s, c]]).astype(np.float32).astype(ml_dtypes.bfloat16)
    pixel = l0[:, None] + 128 * np.arange(8)[None, :]
    angle = 2 * math.pi / G * ((step * (pixel[:, :, None] - PIX // 2) * np.arange(S)) % G)
    c, s = np.cos(angle), np.sin(angle)
    over_x = np.concatenate([np.concatenate([c, -s], 2), np.concatenate([s, c], 2)], 1)
    high, low = split(over_x)
    return over_r, np.concatenate([high, low], 1).reshape(128 * 32, 128)


def column_tables():
    step = G // PIX - 1
    m0 = np.arange(64)
    tile = np.arange(NT)
    angle = 2 * math.pi / 64 * ((step * (m0[:, None] - PIX // 2) * (tile[None, :] - NT)) % 64)
    c, s = np.cos(angle), np.sin(angle)
    over_t = np.concatenate(split(np.block([[c, -s], [s, c]])), 0)
    pixel = m0[:, None] + 64 * np.arange(16)[None, :]
    angle = 2 * math.pi / G * ((step * (pixel[:, :, None] - PIX // 2) * np.arange(128)) % G)
    over_j = np.concatenate([np.cos(angle), -np.sin(angle)], 2) / G
    high, low = split(over_j)
    angle = 2 * math.pi / 64 * ((step * (m0[:, None] - PIX // 2) * (tile[None, :] + 1 - NT)) % 64)
    lone = np.concatenate([np.cos(angle), np.sin(angle)], 0) / G
    return over_t, np.concatenate([high, low], 1).reshape(64 * 32, 256), split(lone)[0]


def iota(shape, axis):
    return lax.broadcasted_iota(jnp.int32, shape, axis)


def dot(a, b):
    return jnp.dot(a, b, preferred_element_type=F32)


def dot_t(a, b):
    return lax.dot_general(a, b, (((1,), (1,)), ((), ())), preferred_element_type=F32)


def fill_slots(samples, dest, cell, plane, skipped):
    column = jnp.bitwise_and(cell, 127)
    mirror = lax.shift_right_logical(column, 6)
    column = jnp.where(mirror == 1, 127 - column, column)
    owner = lax.shift_right_logical(column, 1)
    inner = jnp.bitwise_and(column, 1) + 2 * mirror
    row = dest * 4 + lax.shift_right_logical(cell, 7)
    named = iota((NT, BLK), 0) == owner
    one = jnp.where(named, 1.0, 0.0)
    one_b = one.astype(BF)
    before = jnp.where(iota((BLK, BLK), 0) < iota((BLK, BLK), 1), 1.0, 0.0).astype(BF)
    count = dot(one_b, before)
    rank = jnp.sum(one * count, axis=0, keepdims=True).astype(jnp.int32) - skipped
    here = jnp.logical_and(rank >= 0, rank < CAP)
    slot = jnp.where(here, owner * SLOTS + rank, -1)
    pick = jnp.where(iota((ALL, BLK), 0) == slot, 1.0, 0.0).astype(BF)
    lane = iota((128, BLK), 0)
    kind = lax.shift_right_logical(lane, 5)
    value = jnp.where(kind == 0, row, jnp.where(kind == 1, plane, jnp.where(kind == 2, inner, 1)))
    held = jnp.logical_and(here, jnp.logical_or(kind == 3, jnp.bitwise_and(lane, 31) == rank))
    facts = dot_t(one_b, jnp.where(held, value.astype(F32), 0.0).astype(BF))
    named_most = jnp.max(jnp.sum(one, axis=1, keepdims=True), axis=0, keepdims=True)
    facts = jnp.where(iota((NT, 128), 1) < 112, facts, named_most)
    last = jnp.where(iota((ALL, NT), 0) == iota((ALL, NT), 1) * SLOTS + CAP, 1.0, 0.0).astype(BF)
    slots = dot(pick, samples.astype(BF)) + dot(last, facts.astype(BF))
    return slots.astype(BF)


def exchange_body(first, samples, dest, cell, plane, *rest):
    if first:
        kern_hbm, recv, facts, table, weight, send, send_sem, recv_sem, kern, kern_sem = rest
    else:
        skipped, recv, facts, send, send_sem, recv_sem = rest
    me = lax.axis_index("tile")
    chan = lax.axis_index("chan")
    barrier = pltpu.get_barrier_semaphore()
    fetch = pltpu.make_async_copy(kern_hbm, kern, kern_sem) if first else None
    if first:
        fetch.start()

    def greet(i, _):
        pl.semaphore_signal(
            barrier, inc=1, device_id=(lax.rem(me + i, NT), chan), device_id_type=MESH
        )
        return 0

    lax.fori_loop(1, NT, greet, 0)
    send[...] = fill_slots(samples[...], dest[...], cell[...], plane[...], 0 if first else skipped[...])
    pl.semaphore_wait(barrier, NT - 1)

    def copy(i):
        to = lax.rem(me + i, NT)
        return pltpu.make_async_remote_copy(
            src_ref=send.at[pl.ds(pl.multiple_of(to * SLOTS, SLOTS), SLOTS)],
            dst_ref=recv.at[pl.ds(pl.multiple_of(me * SLOTS, SLOTS), SLOTS)],
            send_sem=send_sem.at[i],
            recv_sem=recv_sem.at[i],
            device_id=(to, chan),
            device_id_type=MESH,
        )

    def start(i, _):
        copy(i).start()
        return 0

    lax.fori_loop(1, NT, start, 0)
    own = pl.ds(pl.multiple_of(me * SLOTS, SLOTS), SLOTS)
    recv[own, :] = send[own, :]
    if first:
        low = iota((S, 128), 1) < S
        mirrored = jnp.where(iota((128, 128), 0) + iota((128, 128), 1) == 191, 1.0, 0.0).astype(BF)

        def prepare(w, _):
            base = pl.multiple_of(w * 128, 128)
            both = kern[pl.ds(base, 128), :].astype(F32)
            real, imag = both[:S], both[S:]
            turned = both.T[:S]
            table[pl.ds(base, S), :] = turned
            swapped = pltpu.roll(turned, S, 1)
            table[pl.ds(base + S, S), :] = jnp.where(low, -swapped, swapped)
            for side in range(2):
                at = base + side * NW * 128
                weight[pl.ds(at, S), :] = jnp.where(low, pltpu.roll(real, S, 1), imag).astype(BF)
                weight[pl.ds(at + S, S), :] = jnp.where(
                    low, -pltpu.roll(imag, S, 1), real
                ).astype(BF)
                if side == 0:
                    both = dot(kern[pl.ds(base, 128), :], mirrored)
                    real, imag = both[:S], both[S:]
            return 0

        fetch.wait()
        lax.fori_loop(0, NW, prepare, 0, unroll=2)

    def wait(i, _):
        copy(i).wait()
        return 0

    lax.fori_loop(1, NT, wait, 0)
    last = jnp.where(iota((NT, ALL), 1) == iota((NT, ALL), 0) * SLOTS + CAP, 1.0, 0.0).astype(BF)
    raw = dot(last, recv[...])
    lane = iota((NT, 128), 1)
    code = (pltpu.roll(raw, 64, 1) * 128.0 + raw) * 32.0 + pltpu.roll(raw, 96, 1)
    facts[...] = jnp.where(lane < SLOTS, code, raw).astype(jnp.int32)


def exchange(first, samples, dest, cell, plane, last):
    vmem = pl.BlockSpec(memory_space=pltpu.VMEM)
    shapes = [jax.ShapeDtypeStruct((ALL, 128), BF), jax.ShapeDtypeStruct((NT, 128), jnp.int32)]
    operands = [samples, dest, cell, plane, last]
    specs = [vmem] * 4 + [pl.BlockSpec(memory_space=pltpu.HBM) if first else vmem]
    scratch = [
        pltpu.VMEM((ALL, 128), BF),
        pltpu.SemaphoreType.DMA((NT,)),
        pltpu.SemaphoreType.DMA((NT,)),
    ]
    if first:
        shapes += [
            jax.ShapeDtypeStruct((NW * 128, 128), F32),
            jax.ShapeDtypeStruct((2 * NW * 128, 128), BF),
        ]
        scratch += [
            pltpu.VMEM((NW * 128, 128), BF),
            pltpu.SemaphoreType.DMA,
        ]
    return pl.pallas_call(
        functools.partial(exchange_body, first),
        out_shape=shapes,
        in_specs=specs,
        out_specs=[vmem] * len(shapes),
        scratch_shapes=scratch,
        compiler_params=pltpu.CompilerParams(
            collective_id=0 if first else 2, has_side_effects=True, vmem_limit_bytes=40 * MIB
        ),
        name="exchange" if first else "exchange_more",
    )(*operands)


def grid_body(facts, recv, table, weight, grid, fill_a, fill_b, todo):
    lane = iota((ALL, 128), 1)
    slot = iota((ALL, 128), 0)
    blocks = jnp.where(jnp.bitwise_and(slot, SLOTS - 1) == CAP, 0.0, recv[...].astype(F32))
    swapped = pltpu.roll(blocks, S, 1)
    fill_a[...] = jnp.where(lane < S, blocks, swapped)
    fill_b[...] = jnp.where(lane < S, swapped, blocks)

    def from_source(t, at):
        part = grid.shape[0] // NT
        grid[pl.ds(pl.multiple_of(t * part, 8), part), :] = jnp.zeros((part, 128), F32)
        for i in range(SLOTS):
            todo[at + i] = facts[t, i] * ALL + t * SLOTS + i
        return at + facts[t, 96]

    number = lax.fori_loop(0, NT, from_source, 0)
    for k in range(TOGETHER):
        todo[number + k] = CAP

    def blocks_together(j, _):
        made = []
        for k in range(TOGETHER):
            code = todo[j * TOGETHER + k]
            i = jnp.bitwise_and(code, ALL - 1)
            fact = lax.shift_right_logical(code, 10)
            base = pl.multiple_of(jnp.bitwise_and(fact, 31) * 128, 128)
            left = (
                fill_a[pl.ds(i, 1), :] * table[pl.ds(base, S), :]
                + fill_b[pl.ds(i, 1), :] * table[pl.ds(base + S, S), :]
            ).astype(BF)
            side = lax.shift_right_logical(fact, 13)
            patch = dot(left, weight[pl.ds(pl.multiple_of(base + side * NW * 128, 128), 128), :])
            made.append((lax.shift_right_logical(fact, 5), patch))
        for place, patch in made:
            at = pl.ds(place * GS, S)
            grid[at, :] = grid[at, :] + patch
        return 0

    lax.fori_loop(0, (number + TOGETHER - 1) // TOGETHER, blocks_together, 0)


def add_blocks(facts, recv, table, weight):
    vmem = pl.BlockSpec(memory_space=pltpu.VMEM)
    return pl.pallas_call(
        grid_body,
        out_shape=jax.ShapeDtypeStruct((512 * GS, 128), F32),
        in_specs=[pl.BlockSpec(memory_space=pltpu.SMEM)] + [vmem] * 3,
        out_specs=vmem,
        scratch_shapes=[
            pltpu.VMEM((ALL, 128), F32),
            pltpu.VMEM((ALL, 128), F32),
            pltpu.SMEM((ALL + 64,), jnp.int32),
        ],
        compiler_params=pltpu.CompilerParams(vmem_limit_bytes=8 * MIB),
        name="add_blocks",
    )(facts, recv, table, weight)


def finish_body(first, grid, facts, over_r, over_x, over_t, lone_t, over_j, *rest):
    if first:
        out, most, *rest, mine, seen, send_y, recv_y = rest
    else:
        out, *rest = rest
    half, pixels, send, recv, wide, middle, alone, lone, fold, last, *sems = rest
    send_a, recv_a, send_b, recv_b, send_c, recv_c = sems
    me = lax.axis_index("tile")
    chan = lax.axis_index("chan")
    home = me // 8
    stays = home == chan
    barrier = pltpu.get_barrier_semaphore()

    def greet(i, _):
        pl.semaphore_signal(
            barrier, inc=1, device_id=(lax.rem(me + i, NT), chan), device_id_type=MESH
        )
        return 0

    lax.fori_loop(1, NT, greet, 0)

    def greet_source(i, _):
        from_t, from_c = chan * 8 + i // NC, lax.rem(i, NC)

        @pl.when(jnp.logical_or(from_t != me, from_c != chan))
        def _():
            pl.semaphore_signal(barrier, inc=1, device_id=(from_t, from_c), device_id_type=MESH)

        return 0

    lax.fori_loop(0, NT, greet_source, 0)
    greeted = 2 * NT - 1
    if first:
        greeted += NC - 1
        for i in range(1, NC):
            pl.semaphore_signal(
                barrier, inc=1, device_id=(me, lax.rem(chan + i, NC)), device_id_type=MESH
            )

    def over_rows(x, _):
        part = [grid[pl.ds(i * 128 * GS + x, 128, stride=GS), :] for i in range(4)]
        real = jnp.concatenate([p[:, :S] for p in part], axis=1)
        imag = jnp.concatenate([p[:, S:] for p in part], axis=1)
        got = dot(over_r[...], jnp.concatenate([real, imag], axis=0).astype(BF))
        half[pl.ds(x, 128, stride=HS), :] = got[:128, :128]
        half[pl.ds(S + x, 128, stride=HS), :] = got[128:, :128]
        half[pl.ds(128 * HS + x, 128, stride=HS), :] = got[:128, 128:]
        half[pl.ds(128 * HS + S + x, 128, stride=HS), :] = got[128:, 128:]
        return 0

    lax.fori_loop(0, S, over_rows, 0, unroll=32)

    def give_rows(to):
        return pltpu.make_async_remote_copy(
            src_ref=send.at[pl.ds(pl.multiple_of(to * 64, 64), 64)],
            dst_ref=recv.at[pl.ds(pl.multiple_of(me * 64, 64), 64)],
            send_sem=send_a.at[to],
            recv_sem=recv_a.at[me],
            device_id=(to, chan),
            device_id_type=MESH,
        )

    def take_rows(source):
        at = pl.ds(pl.multiple_of(source * 64, 64), 64)
        return pltpu.make_async_remote_copy(
            src_ref=recv.at[at],
            dst_ref=recv.at[at],
            send_sem=send_a.at[source],
            recv_sem=recv_a.at[source],
            device_id=(source, chan),
            device_id_type=MESH,
        )

    def give_alone(to):
        return pltpu.make_async_remote_copy(
            src_ref=alone.at[to],
            dst_ref=lone.at[me],
            send_sem=send_c.at[to],
            recv_sem=recv_c.at[me],
            device_id=(to, chan),
            device_id_type=MESH,
        )

    def take_alone(source):
        return pltpu.make_async_remote_copy(
            src_ref=lone.at[source],
            dst_ref=lone.at[source],
            send_sem=send_c.at[source],
            recv_sem=recv_c.at[source],
            device_id=(source, chan),
            device_id_type=MESH,
        )

    def over_offsets(l0):
        at = l0 * HS
        right = jnp.concatenate(
            [half[pl.ds(at, 128), :], half[pl.ds(128 * HS + at, 128), :]], axis=1
        ).astype(BF)
        got = dot(over_x[pl.ds(pl.multiple_of(l0 * 32, 32), 32), :], right)
        got = got[:16] + got[16:]
        turned = pltpu.roll(got[:, 128:], 1, 1)
        for q in range(2):
            rows = slice(8 * q, 8 * q + 8)
            pixels[pl.ds(2 * l0 + q, 8, stride=256), :] = got[rows, :128]
            pixels[pl.ds(2048 + 2 * l0 + q, 8, stride=256), :] = (
                turned[rows] if q == 0 else -turned[rows]
            )

    past = iota((64, 128), 1) > 0
    lane = iota((32, 128), 1)
    place = iota((32, 128), 0)

    def pack(i, part):
        to = jnp.bitwise_and(i + me // 4, 7) * 4 + part
        rows = pl.multiple_of(to * 64, 64)
        mirror = pixels[pl.ds(2048 + rows, 64), :]
        send[pl.ds(rows, 64), :] = (
            pixels[pl.ds(rows, 64), :] + jnp.where(past, mirror, 0.0)
        ).astype(BF)
        spread = jnp.zeros((32, 128), F32)
        for q in range(2):
            column = pixels[pl.ds(2048 + rows + q, 32, stride=2), :][:, :1]
            spread = jnp.where(
                lane == place + 32 * q, jnp.broadcast_to(column, (32, 128)), spread
            )
        alone[to] = jnp.sum(spread, axis=0, keepdims=True)
        return part

    def start(i, part):
        to = jnp.bitwise_and(i + me // 4, 7) * 4 + part

        @pl.when(to != me)
        def _():
            give_rows(to).start()
            give_alone(to).start()

        return part

    for turn in range(4):
        part = jnp.bitwise_and(me + turn, 3)

        def some(j, part):
            for k in range(16):
                over_offsets(part * 32 + j * 16 + k)
            return part

        lax.fori_loop(0, 2, some, part)
        lax.fori_loop(0, 8, pack, part, unroll=8)
        if turn == 0:
            pl.semaphore_wait(barrier, jnp.where(stays, greeted - 1, greeted))
        lax.fori_loop(0, 8, start, part)
    if first:
        known = jnp.where(iota((NT, 128), 1) < 112, 0, facts[...]).astype(F32)
        known = jnp.max(jnp.max(known, axis=0, keepdims=True), axis=1, keepdims=True)
        mine[...] = jnp.broadcast_to(known, (8, 128))

        def tell(i):
            return pltpu.make_async_remote_copy(
                src_ref=mine,
                dst_ref=seen.at[i],
                send_sem=send_y.at[i],
                recv_sem=recv_y.at[i],
                device_id=(me, lax.rem(chan + i, NC)),
                device_id_type=MESH,
            )

        for i in range(1, NC):
            tell(i).start()
    own = pl.ds(pl.multiple_of(me * 64, 64), 64)
    recv[own, :] = send[own, :]
    lone[me] = alone[me]

    def wait(i, _):
        take_rows(lax.rem(me + i, NT)).wait_recv()
        take_alone(lax.rem(me + i, NT)).wait_recv()
        return 0

    lax.fori_loop(1, NT, wait, 0)

    def widen(t, _):
        block = recv[pl.ds(pl.multiple_of(t * 64, 64), 64), :].astype(F32)
        wide[pl.ds(t * WS, 64), :] = block
        return 0

    lax.fori_loop(0, NT, widen, 0, unroll=4)

    def over_tiles(l, _):
        rows = [wide[pl.ds(2 * l + q, NT, stride=WS), :] for q in range(2)]
        got = dot(over_t[...], jnp.concatenate(rows, axis=0).astype(BF))
        middle[pl.ds(l * MS, 128), :] = got[:128] + got[128:]
        return 0

    lax.fori_loop(0, 32, over_tiles, 0, unroll=8)
    added = dot(lone_t[...], lone[...].reshape(NT, 128).astype(BF))
    wide[0:64, :] = added[:64] - pltpu.roll(added[64:], 96, 1)

    def over_columns(a, h):
        made = []
        for b in range(4):
            m0 = h * 32 + b * 8 + a
            right = jnp.concatenate(
                [middle[pl.ds(64 * q + m0, 32, stride=MS), :] for q in range(2)], axis=1
            )
            high = right.astype(BF)
            low = (right - high.astype(F32)).astype(BF)
            left = over_j[pl.ds(pl.multiple_of(m0 * 32, 32), 32), :]
            got = dot_t(left, high)
            got = got[:16] + got[16:] + dot_t(left[:16], low)
            made.append(got + wide[pl.ds(m0, 1), :][:, :32])
        fold[pl.ds(h * 8 + a, 16, stride=16), :] = jnp.concatenate(made, axis=1)
        return h

    slot = lax.rem(me, 8) * NC + chan

    def give(to):
        return pltpu.make_async_remote_copy(
            src_ref=fold.at[pl.ds(pl.multiple_of(to * 8, 8), 8)],
            dst_ref=last.at[pl.ds(pl.multiple_of(slot * 8, 8), 8)],
            send_sem=send_b.at[to],
            recv_sem=recv_b.at[slot],
            device_id=(to, home),
            device_id_type=MESH,
        )

    def take(i):
        at = pl.ds(pl.multiple_of(i * 8, 8), 8)
        return pltpu.make_async_remote_copy(
            src_ref=last.at[at],
            dst_ref=last.at[at],
            send_sem=send_b.at[i],
            recv_sem=recv_b.at[i],
            device_id=(chan * 8 + i // NC, lax.rem(i, NC)),
            device_id_type=MESH,
        )

    def start_b(i, h):
        to = 2 * jnp.bitwise_and(i + me // 2, 15) + h

        @pl.when(jnp.logical_or(jnp.logical_not(stays), to != me))
        def _():
            give(to).start()

        return h

    for h in range(2):
        lax.fori_loop(0, 8, over_columns, h, unroll=4)
        lax.fori_loop(0, 16, start_b, h)

    @pl.when(stays)
    def _():
        last[pl.ds(pl.multiple_of(slot * 8, 8), 8), :] = fold[
            pl.ds(pl.multiple_of(me * 8, 8), 8), :
        ]

    if first:
        for i in range(1, NC):
            tell(i).wait()
            known = jnp.maximum(known, jnp.max(seen[i][:1], axis=1, keepdims=True))
        most[0, 0] = jnp.max(known)

    def wait_b(i, _):
        @pl.when(jnp.logical_or(jnp.logical_not(stays), i != slot))
        def _():
            take(i).wait_recv()

        return 0

    lax.fori_loop(0, NT, wait_b, 0)
    totals = []
    for t in range(8):
        total = last[t * 32 : t * 32 + 8, :]
        for c in range(1, NC):
            total = total + last[t * 32 + c * 8 : t * 32 + c * 8 + 8, :]
        totals.append(total)
    for b in range(4):
        out[b * 8 : b * 8 + 8, :] = jnp.concatenate(
            [total[:, b * 32 : b * 32 + 32] for total in totals], axis=1
        )

    def sent_b(i, _):
        @pl.when(jnp.logical_or(jnp.logical_not(stays), i != me))
        def _():
            give(i).wait_send()

        return 0

    lax.fori_loop(0, NT, sent_b, 0)

    def sent_a(i, _):
        give_rows(lax.rem(me + i, NT)).wait_send()
        give_alone(lax.rem(me + i, NT)).wait_send()
        return 0

    lax.fori_loop(1, NT, sent_a, 0)


def finish(first, grid, facts, over_r, over_x, over_t, lone_t, over_j):
    vmem = pl.BlockSpec(memory_space=pltpu.VMEM)
    shapes, outs = [jax.ShapeDtypeStruct((32, 256), F32)], [vmem]
    scratch = [
        pltpu.VMEM((2 * 128 * HS, 128), F32),
        pltpu.VMEM((4096, 128), F32),
        pltpu.VMEM((NT * 64, 128), BF),
        pltpu.VMEM((NT * 64, 128), BF),
        pltpu.VMEM((NT * WS, 128), F32),
        pltpu.VMEM((32 * MS, 128), F32),
        pltpu.VMEM((NT, 1, 128), F32),
        pltpu.VMEM((NT, 1, 128), F32),
        pltpu.VMEM((256, 128), F32),
        pltpu.VMEM((256, 128), F32),
        pltpu.SemaphoreType.DMA((NT,)),
        pltpu.SemaphoreType.DMA((NT,)),
        pltpu.SemaphoreType.DMA((NT,)),
        pltpu.SemaphoreType.DMA((NT,)),
        pltpu.SemaphoreType.DMA((NT,)),
        pltpu.SemaphoreType.DMA((NT,)),
    ]
    if first:
        shapes.append(jax.ShapeDtypeStruct((1, 1), F32))
        outs.append(pl.BlockSpec(memory_space=pltpu.SMEM))
        scratch += [
            pltpu.VMEM((8, 128), F32),
            pltpu.VMEM((NC, 8, 128), F32),
            pltpu.SemaphoreType.DMA((NC,)),
            pltpu.SemaphoreType.DMA((NC,)),
        ]
    return pl.pallas_call(
        functools.partial(finish_body, first),
        out_shape=shapes,
        in_specs=[vmem] * 7,
        out_specs=outs,
        scratch_shapes=scratch,
        compiler_params=pltpu.CompilerParams(
            collective_id=1 if first else 3, has_side_effects=True, vmem_limit_bytes=30 * MIB
        ),
        name="finish" if first else "finish_more",
    )(grid, facts, over_r, over_x, over_t, lone_t, over_j)


def local(visibilities, kernels, destination, cell, plane):
    over_r, over_x = (jnp.asarray(t) for t in row_tables())
    over_t, over_j, lone_t = (jnp.asarray(t) for t in column_tables())
    samples = visibilities[0]
    dest = destination.reshape(1, BLK)
    kern = kernels.reshape(NW * 128, 128)
    recv, facts, table, weight = exchange(True, samples, dest, cell, plane, kern)
    grid = add_blocks(facts, recv, table, weight)
    image, most = finish(True, grid, facts, over_r, over_x, over_t, lone_t, over_j)
    most = most[0, 0]

    def more(image):
        def again(state):
            done, total = state
            skipped = jnp.broadcast_to(done, (1, BLK))
            recv, facts = exchange(False, samples, dest, cell, plane, skipped)
            grid = add_blocks(facts, recv, table, weight)
            [terms] = finish(False, grid, facts, over_r, over_x, over_t, lone_t, over_j)
            return done + CAP, total + terms

        return lax.while_loop(
            lambda state: state[0].astype(F32) < most, again, (jnp.int32(CAP), image)
        )[1]

    image = lax.cond(most > CAP, more, lambda terms: terms, image)
    return image.T


def solution(mesh):
    placed = (
        P("chan", "tile", None),
        P("chan", None, None, None, None),
        P("chan", "tile", None),
        P("chan", "tile"),
        P("chan", "tile"),
    )
    return jax.shard_map(
        local, mesh=mesh, in_specs=placed, out_specs=P("chan", "tile"), check_vma=False
    )
```

```python
import functools
import math

import jax
import jax.numpy as jnp
import ml_dtypes
import numpy as np
from jax import lax
from jax.experimental import pallas as pl
from jax.experimental.pallas import tpu as pltpu
from jax.sharding import PartitionSpec as P

G = 8192
S = 64
NW = 32
PIX = 1024
NT = 32
NC = 4
BLK = 256
CAP = 31
GS = 65
HS = 129
TOGETHER = 48
WS = 65
MS = 129
SLOTS = 32
ALL = NT * SLOTS
MIB = 1 << 20
BF = jnp.bfloat16
F32 = jnp.float32
MESH = pl.DeviceIdType.MESH


def split(table):
    high = table.astype(np.float32).astype(ml_dtypes.bfloat16)
    low = (table - high.astype(np.float64)).astype(ml_dtypes.bfloat16)
    return high, low


def row_tables():
    step = G // PIX - 1
    l0 = np.arange(128)
    angle = 2 * math.pi / 128 * ((step * (l0[:, None] - PIX // 2) * (l0[None, :] - 64)) % 128)
    c, s = np.cos(angle), np.sin(angle)
    over_r = np.block([[c, -s], [s, c]]).astype(np.float32).astype(ml_dtypes.bfloat16)
    pixel = l0[:, None] + 128 * np.arange(8)[None, :]
    angle = 2 * math.pi / G * ((step * (pixel[:, :, None] - PIX // 2) * np.arange(S)) % G)
    c, s = np.cos(angle), np.sin(angle)
    over_x = np.concatenate([np.concatenate([c, -s], 2), np.concatenate([s, c], 2)], 1)
    high, low = split(over_x)
    return over_r, np.concatenate([high, low], 1).reshape(128 * 32, 128)


def column_tables():
    step = G // PIX - 1
    m0 = np.arange(64)
    tile = np.arange(NT)
    angle = 2 * math.pi / 64 * ((step * (m0[:, None] - PIX // 2) * (tile[None, :] - NT)) % 64)
    c, s = np.cos(angle), np.sin(angle)
    over_t = np.concatenate(split(np.block([[c, -s], [s, c]])), 0)
    pixel = m0[:, None] + 64 * np.arange(16)[None, :]
    angle = 2 * math.pi / G * ((step * (pixel[:, :, None] - PIX // 2) * np.arange(128)) % G)
    over_j = np.concatenate([np.cos(angle), -np.sin(angle)], 2) / G
    high, low = split(over_j)
    angle = 2 * math.pi / 64 * ((step * (m0[:, None] - PIX // 2) * (tile[None, :] + 1 - NT)) % 64)
    lone = np.concatenate([np.cos(angle), np.sin(angle)], 0) / G
    return over_t, np.concatenate([high, low], 1).reshape(64 * 32, 256), split(lone)[0]


def iota(shape, axis):
    return lax.broadcasted_iota(jnp.int32, shape, axis)


def dot(a, b):
    return jnp.dot(a, b, preferred_element_type=F32)


def dot_t(a, b):
    return lax.dot_general(a, b, (((1,), (1,)), ((), ())), preferred_element_type=F32)


def fill_slots(samples, dest, cell, plane, skipped):
    column = jnp.bitwise_and(cell, 127)
    mirror = lax.shift_right_logical(column, 6)
    column = jnp.where(mirror == 1, 127 - column, column)
    owner = lax.shift_right_logical(column, 1)
    inner = jnp.bitwise_and(column, 1) + 2 * mirror
    row = dest * 4 + lax.shift_right_logical(cell, 7)
    named = iota((NT, BLK), 0) == owner
    one = jnp.where(named, 1.0, 0.0)
    one_b = one.astype(BF)
    before = jnp.where(iota((BLK, BLK), 0) < iota((BLK, BLK), 1), 1.0, 0.0).astype(BF)
    count = dot(one_b, before)
    rank = jnp.sum(one * count, axis=0, keepdims=True).astype(jnp.int32) - skipped
    here = jnp.logical_and(rank >= 0, rank < CAP)
    slot = jnp.where(here, owner * SLOTS + rank, -1)
    pick = jnp.where(iota((ALL, BLK), 0) == slot, 1.0, 0.0).astype(BF)
    lane = iota((128, BLK), 0)
    kind = lax.shift_right_logical(lane, 5)
    value = jnp.where(kind == 0, row, jnp.where(kind == 1, plane, jnp.where(kind == 2, inner, 1)))
    held = jnp.logical_and(here, jnp.logical_or(kind == 3, jnp.bitwise_and(lane, 31) == rank))
    facts = dot_t(one_b, jnp.where(held, value.astype(F32), 0.0).astype(BF))
    named_most = jnp.max(jnp.sum(one, axis=1, keepdims=True), axis=0, keepdims=True)
    facts = jnp.where(iota((NT, 128), 1) < 112, facts, named_most)
    last = jnp.where(iota((ALL, NT), 0) == iota((ALL, NT), 1) * SLOTS + CAP, 1.0, 0.0).astype(BF)
    slots = dot(pick, samples.astype(BF)) + dot(last, facts.astype(BF))
    return slots.astype(BF)


def exchange_body(first, samples, dest, cell, plane, *rest):
    if first:
        kern_hbm, recv, facts, table, weight, send, send_sem, recv_sem, kern, kern_sem = rest
    else:
        skipped, recv, facts, send, send_sem, recv_sem = rest
    me = lax.axis_index("tile")
    chan = lax.axis_index("chan")
    barrier = pltpu.get_barrier_semaphore()
    fetch = pltpu.make_async_copy(kern_hbm, kern, kern_sem) if first else None
    if first:
        fetch.start()

    def greet(i, _):
        pl.semaphore_signal(
            barrier, inc=1, device_id=(lax.rem(me + i, NT), chan), device_id_type=MESH
        )
        return 0

    lax.fori_loop(1, NT, greet, 0)
    send[...] = fill_slots(samples[...], dest[...], cell[...], plane[...], 0 if first else skipped[...])
    pl.semaphore_wait(barrier, NT - 1)

    def copy(i):
        to = lax.rem(me + i, NT)
        return pltpu.make_async_remote_copy(
            src_ref=send.at[pl.ds(pl.multiple_of(to * SLOTS, SLOTS), SLOTS)],
            dst_ref=recv.at[pl.ds(pl.multiple_of(me * SLOTS, SLOTS), SLOTS)],
            send_sem=send_sem.at[i],
            recv_sem=recv_sem.at[i],
            device_id=(to, chan),
            device_id_type=MESH,
        )

    def start(i, _):
        copy(i).start()
        return 0

    lax.fori_loop(1, NT, start, 0)
    own = pl.ds(pl.multiple_of(me * SLOTS, SLOTS), SLOTS)
    recv[own, :] = send[own, :]
    if first:
        low = iota((S, 128), 1) < S
        mirrored = jnp.where(iota((128, 128), 0) + iota((128, 128), 1) == 191, 1.0, 0.0).astype(BF)

        def prepare(w, _):
            base = pl.multiple_of(w * 128, 128)
            both = kern[pl.ds(base, 128), :].astype(F32)
            real, imag = both[:S], both[S:]
            turned = both.T[:S]
            table[pl.ds(base, S), :] = turned
            swapped = pltpu.roll(turned, S, 1)
            table[pl.ds(base + S, S), :] = jnp.where(low, -swapped, swapped)
            for side in range(2):
                at = base + side * NW * 128
                weight[pl.ds(at, S), :] = jnp.where(low, pltpu.roll(real, S, 1), imag).astype(BF)
                weight[pl.ds(at + S, S), :] = jnp.where(
                    low, -pltpu.roll(imag, S, 1), real
                ).astype(BF)
                if side == 0:
                    both = dot(kern[pl.ds(base, 128), :], mirrored)
                    real, imag = both[:S], both[S:]
            return 0

        fetch.wait()
        lax.fori_loop(0, NW, prepare, 0, unroll=4)

    def wait(i, _):
        copy(i).wait()
        return 0

    lax.fori_loop(1, NT, wait, 0)
    last = jnp.where(iota((NT, ALL), 1) == iota((NT, ALL), 0) * SLOTS + CAP, 1.0, 0.0).astype(BF)
    raw = dot(last, recv[...])
    lane = iota((NT, 128), 1)
    code = (pltpu.roll(raw, 64, 1) * 128.0 + raw) * 32.0 + pltpu.roll(raw, 96, 1)
    facts[...] = jnp.where(lane < SLOTS, code, raw).astype(jnp.int32)


def exchange(first, samples, dest, cell, plane, last):
    vmem = pl.BlockSpec(memory_space=pltpu.VMEM)
    shapes = [jax.ShapeDtypeStruct((ALL, 128), BF), jax.ShapeDtypeStruct((NT, 128), jnp.int32)]
    operands = [samples, dest, cell, plane, last]
    specs = [vmem] * 4 + [pl.BlockSpec(memory_space=pltpu.HBM) if first else vmem]
    scratch = [
        pltpu.VMEM((ALL, 128), BF),
        pltpu.SemaphoreType.DMA((NT,)),
        pltpu.SemaphoreType.DMA((NT,)),
    ]
    if first:
        shapes += [
            jax.ShapeDtypeStruct((NW * 128, 128), F32),
            jax.ShapeDtypeStruct((2 * NW * 128, 128), BF),
        ]
        scratch += [
            pltpu.VMEM((NW * 128, 128), BF),
            pltpu.SemaphoreType.DMA,
        ]
    return pl.pallas_call(
        functools.partial(exchange_body, first),
        out_shape=shapes,
        in_specs=specs,
        out_specs=[vmem] * len(shapes),
        scratch_shapes=scratch,
        compiler_params=pltpu.CompilerParams(
            collective_id=0 if first else 2, has_side_effects=True, vmem_limit_bytes=40 * MIB
        ),
        name="exchange" if first else "exchange_more",
    )(*operands)


def grid_body(facts, recv, table, weight, grid, fill_a, fill_b, todo):
    lane = iota((ALL, 128), 1)
    slot = iota((ALL, 128), 0)
    blocks = jnp.where(jnp.bitwise_and(slot, SLOTS - 1) == CAP, 0.0, recv[...].astype(F32))
    swapped = pltpu.roll(blocks, S, 1)
    fill_a[...] = jnp.where(lane < S, blocks, swapped)
    fill_b[...] = jnp.where(lane < S, swapped, blocks)

    def from_source(t, at):
        part = grid.shape[0] // NT
        grid[pl.ds(pl.multiple_of(t * part, 8), part), :] = jnp.zeros((part, 128), F32)
        for i in range(SLOTS):
            todo[at + i] = facts[t, i] * ALL + t * SLOTS + i
        return at + facts[t, 96]

    number = lax.fori_loop(0, NT, from_source, 0)
    for k in range(TOGETHER):
        todo[number + k] = CAP

    def blocks_together(j, _):
        made = []
        for k in range(TOGETHER):
            code = todo[j * TOGETHER + k]
            i = jnp.bitwise_and(code, ALL - 1)
            fact = lax.shift_right_logical(code, 10)
            base = pl.multiple_of(jnp.bitwise_and(fact, 31) * 128, 128)
            left = (
                fill_a[pl.ds(i, 1), :] * table[pl.ds(base, S), :]
                + fill_b[pl.ds(i, 1), :] * table[pl.ds(base + S, S), :]
            ).astype(BF)
            side = lax.shift_right_logical(fact, 13)
            patch = dot(left, weight[pl.ds(pl.multiple_of(base + side * NW * 128, 128), 128), :])
            made.append((lax.shift_right_logical(fact, 5), patch))
        for place, patch in made:
            at = pl.ds(place * GS, S)
            grid[at, :] = grid[at, :] + patch
        return 0

    lax.fori_loop(0, (number + TOGETHER - 1) // TOGETHER, blocks_together, 0)


def add_blocks(facts, recv, table, weight):
    vmem = pl.BlockSpec(memory_space=pltpu.VMEM)
    return pl.pallas_call(
        grid_body,
        out_shape=jax.ShapeDtypeStruct((512 * GS, 128), F32),
        in_specs=[pl.BlockSpec(memory_space=pltpu.SMEM)] + [vmem] * 3,
        out_specs=vmem,
        scratch_shapes=[
            pltpu.VMEM((ALL, 128), F32),
            pltpu.VMEM((ALL, 128), F32),
            pltpu.SMEM((ALL + 64,), jnp.int32),
        ],
        compiler_params=pltpu.CompilerParams(vmem_limit_bytes=8 * MIB),
        name="add_blocks",
    )(facts, recv, table, weight)


def finish_body(first, grid, facts, over_r, over_x, over_t, lone_t, over_j, *rest):
    if first:
        out, most, *rest, mine, seen, send_y, recv_y = rest
    else:
        out, *rest = rest
    half, pixels, send, recv, wide, middle, alone, lone, fold, last, *sems = rest
    send_a, recv_a, send_b, recv_b, send_c, recv_c = sems
    me = lax.axis_index("tile")
    chan = lax.axis_index("chan")
    home = me // 8
    stays = home == chan
    barrier = pltpu.get_barrier_semaphore()

    def greet(i, _):
        pl.semaphore_signal(
            barrier, inc=1, device_id=(lax.rem(me + i, NT), chan), device_id_type=MESH
        )
        return 0

    lax.fori_loop(1, NT, greet, 0)

    def greet_source(i, _):
        from_t, from_c = chan * 8 + i // NC, lax.rem(i, NC)

        @pl.when(jnp.logical_or(from_t != me, from_c != chan))
        def _():
            pl.semaphore_signal(barrier, inc=1, device_id=(from_t, from_c), device_id_type=MESH)

        return 0

    lax.fori_loop(0, NT, greet_source, 0)
    greeted = 2 * NT - 1
    if first:
        greeted += NC - 1
        for i in range(1, NC):
            pl.semaphore_signal(
                barrier, inc=1, device_id=(me, lax.rem(chan + i, NC)), device_id_type=MESH
            )

    def over_rows(x, _):
        part = [grid[pl.ds(i * 128 * GS + x, 128, stride=GS), :] for i in range(4)]
        real = jnp.concatenate([p[:, :S] for p in part], axis=1)
        imag = jnp.concatenate([p[:, S:] for p in part], axis=1)
        got = dot(over_r[...], jnp.concatenate([real, imag], axis=0).astype(BF))
        half[pl.ds(x, 128, stride=HS), :] = got[:128, :128]
        half[pl.ds(S + x, 128, stride=HS), :] = got[128:, :128]
        half[pl.ds(128 * HS + x, 128, stride=HS), :] = got[:128, 128:]
        half[pl.ds(128 * HS + S + x, 128, stride=HS), :] = got[128:, 128:]
        return 0

    lax.fori_loop(0, S, over_rows, 0, unroll=32)

    def give_rows(to):
        return pltpu.make_async_remote_copy(
            src_ref=send.at[pl.ds(pl.multiple_of(to * 64, 64), 64)],
            dst_ref=recv.at[pl.ds(pl.multiple_of(me * 64, 64), 64)],
            send_sem=send_a.at[to],
            recv_sem=recv_a.at[me],
            device_id=(to, chan),
            device_id_type=MESH,
        )

    def take_rows(source):
        at = pl.ds(pl.multiple_of(source * 64, 64), 64)
        return pltpu.make_async_remote_copy(
            src_ref=recv.at[at],
            dst_ref=recv.at[at],
            send_sem=send_a.at[source],
            recv_sem=recv_a.at[source],
            device_id=(source, chan),
            device_id_type=MESH,
        )

    def give_alone(to):
        return pltpu.make_async_remote_copy(
            src_ref=alone.at[to],
            dst_ref=lone.at[me],
            send_sem=send_c.at[to],
            recv_sem=recv_c.at[me],
            device_id=(to, chan),
            device_id_type=MESH,
        )

    def take_alone(source):
        return pltpu.make_async_remote_copy(
            src_ref=lone.at[source],
            dst_ref=lone.at[source],
            send_sem=send_c.at[source],
            recv_sem=recv_c.at[source],
            device_id=(source, chan),
            device_id_type=MESH,
        )

    def over_offsets(l0):
        at = l0 * HS
        right = jnp.concatenate(
            [half[pl.ds(at, 128), :], half[pl.ds(128 * HS + at, 128), :]], axis=1
        ).astype(BF)
        got = dot(over_x[pl.ds(pl.multiple_of(l0 * 32, 32), 32), :], right)
        got = got[:16] + got[16:]
        turned = pltpu.roll(got[:, 128:], 1, 1)
        for q in range(2):
            rows = slice(8 * q, 8 * q + 8)
            pixels[pl.ds(2 * l0 + q, 8, stride=256), :] = got[rows, :128]
            pixels[pl.ds(2048 + 2 * l0 + q, 8, stride=256), :] = (
                turned[rows] if q == 0 else -turned[rows]
            )

    past = iota((64, 128), 1) > 0
    lane = iota((32, 128), 1)
    place = iota((32, 128), 0)

    def pack(i, part):
        to = jnp.bitwise_and(i + me // 4, 7) * 4 + part
        rows = pl.multiple_of(to * 64, 64)
        mirror = pixels[pl.ds(2048 + rows, 64), :]
        send[pl.ds(rows, 64), :] = (
            pixels[pl.ds(rows, 64), :] + jnp.where(past, mirror, 0.0)
        ).astype(BF)
        spread = jnp.zeros((32, 128), F32)
        for q in range(2):
            column = pixels[pl.ds(2048 + rows + q, 32, stride=2), :][:, :1]
            spread = jnp.where(
                lane == place + 32 * q, jnp.broadcast_to(column, (32, 128)), spread
            )
        alone[to] = jnp.sum(spread, axis=0, keepdims=True)
        return part

    def start(i, part):
        to = jnp.bitwise_and(i + me // 4, 7) * 4 + part

        @pl.when(to != me)
        def _():
            give_rows(to).start()
            give_alone(to).start()

        return part

    for turn in range(4):
        part = jnp.bitwise_and(me + turn, 3)

        def some(j, part):
            for k in range(16):
                over_offsets(part * 32 + j * 16 + k)
            return part

        lax.fori_loop(0, 2, some, part)
        lax.fori_loop(0, 8, pack, part, unroll=8)
        if turn == 0:
            pl.semaphore_wait(barrier, jnp.where(stays, greeted - 1, greeted))
        lax.fori_loop(0, 8, start, part, unroll=True)
    if first:
        known = jnp.where(iota((NT, 128), 1) < 112, 0, facts[...]).astype(F32)
        known = jnp.max(jnp.max(known, axis=0, keepdims=True), axis=1, keepdims=True)
        mine[...] = jnp.broadcast_to(known, (8, 128))

        def tell(i):
            return pltpu.make_async_remote_copy(
                src_ref=mine,
                dst_ref=seen.at[i],
                send_sem=send_y.at[i],
                recv_sem=recv_y.at[i],
                device_id=(me, lax.rem(chan + i, NC)),
                device_id_type=MESH,
            )

        for i in range(1, NC):
            tell(i).start()
    own = pl.ds(pl.multiple_of(me * 64, 64), 64)
    recv[own, :] = send[own, :]
    lone[me] = alone[me]

    def wait(i, _):
        take_rows(lax.rem(me + i, NT)).wait_recv()
        take_alone(lax.rem(me + i, NT)).wait_recv()
        return 0

    lax.fori_loop(1, NT, wait, 0)

    def widen(t, _):
        block = recv[pl.ds(pl.multiple_of(t * 64, 64), 64), :].astype(F32)
        wide[pl.ds(t * WS, 64), :] = block
        return 0

    lax.fori_loop(0, NT, widen, 0, unroll=16)

    def over_tiles(l, _):
        rows = [wide[pl.ds(2 * l + q, NT, stride=WS), :] for q in range(2)]
        got = dot(over_t[...], jnp.concatenate(rows, axis=0).astype(BF))
        middle[pl.ds(l * MS, 128), :] = got[:128] + got[128:]
        return 0

    lax.fori_loop(0, 32, over_tiles, 0, unroll=32)
    added = dot(lone_t[...], lone[...].reshape(NT, 128).astype(BF))
    wide[0:64, :] = added[:64] - pltpu.roll(added[64:], 96, 1)

    def over_columns(a, h):
        made = []
        for b in range(4):
            m0 = h * 32 + b * 8 + a
            right = jnp.concatenate(
                [middle[pl.ds(64 * q + m0, 32, stride=MS), :] for q in range(2)], axis=1
            )
            high = right.astype(BF)
            low = (right - high.astype(F32)).astype(BF)
            left = over_j[pl.ds(pl.multiple_of(m0 * 32, 32), 32), :]
            got = dot_t(left, high)
            got = got[:16] + got[16:] + dot_t(left[:16], low)
            made.append(got + wide[pl.ds(m0, 1), :][:, :32])
        fold[pl.ds(h * 8 + a, 16, stride=16), :] = jnp.concatenate(made, axis=1)
        return h

    slot = lax.rem(me, 8) * NC + chan

    def give(to):
        return pltpu.make_async_remote_copy(
            src_ref=fold.at[pl.ds(pl.multiple_of(to * 8, 8), 8)],
            dst_ref=last.at[pl.ds(pl.multiple_of(slot * 8, 8), 8)],
            send_sem=send_b.at[to],
            recv_sem=recv_b.at[slot],
            device_id=(to, home),
            device_id_type=MESH,
        )

    def take(i):
        at = pl.ds(pl.multiple_of(i * 8, 8), 8)
        return pltpu.make_async_remote_copy(
            src_ref=last.at[at],
            dst_ref=last.at[at],
            send_sem=send_b.at[i],
            recv_sem=recv_b.at[i],
            device_id=(chan * 8 + i // NC, lax.rem(i, NC)),
            device_id_type=MESH,
        )

    def start_b(i, h):
        to = 2 * jnp.bitwise_and(i + me // 2, 15) + h

        @pl.when(jnp.logical_or(jnp.logical_not(stays), to != me))
        def _():
            give(to).start()

        return h

    for h in range(2):
        lax.fori_loop(0, 8, over_columns, h, unroll=8)
        lax.fori_loop(0, 16, start_b, h, unroll=8)

    @pl.when(stays)
    def _():
        last[pl.ds(pl.multiple_of(slot * 8, 8), 8), :] = fold[
            pl.ds(pl.multiple_of(me * 8, 8), 8), :
        ]

    if first:
        for i in range(1, NC):
            tell(i).wait()
            known = jnp.maximum(known, jnp.max(seen[i][:1], axis=1, keepdims=True))
        most[0, 0] = jnp.max(known)

    def wait_b(i, _):
        @pl.when(jnp.logical_or(jnp.logical_not(stays), i != slot))
        def _():
            take(i).wait_recv()

        return 0

    lax.fori_loop(0, NT, wait_b, 0)
    totals = []
    for t in range(8):
        total = last[t * 32 : t * 32 + 8, :]
        for c in range(1, NC):
            total = total + last[t * 32 + c * 8 : t * 32 + c * 8 + 8, :]
        totals.append(total)
    for b in range(4):
        out[b * 8 : b * 8 + 8, :] = jnp.concatenate(
            [total[:, b * 32 : b * 32 + 32] for total in totals], axis=1
        )

    def sent_b(i, _):
        @pl.when(jnp.logical_or(jnp.logical_not(stays), i != me))
        def _():
            give(i).wait_send()

        return 0

    lax.fori_loop(0, NT, sent_b, 0)

    def sent_a(i, _):
        give_rows(lax.rem(me + i, NT)).wait_send()
        give_alone(lax.rem(me + i, NT)).wait_send()
        return 0

    lax.fori_loop(1, NT, sent_a, 0)


def finish(first, grid, facts, over_r, over_x, over_t, lone_t, over_j):
    vmem = pl.BlockSpec(memory_space=pltpu.VMEM)
    shapes, outs = [jax.ShapeDtypeStruct((32, 256), F32)], [vmem]
    scratch = [
        pltpu.VMEM((2 * 128 * HS, 128), F32),
        pltpu.VMEM((4096, 128), F32),
        pltpu.VMEM((NT * 64, 128), BF),
        pltpu.VMEM((NT * 64, 128), BF),
        pltpu.VMEM((NT * WS, 128), F32),
        pltpu.VMEM((32 * MS, 128), F32),
        pltpu.VMEM((NT, 1, 128), F32),
        pltpu.VMEM((NT, 1, 128), F32),
        pltpu.VMEM((256, 128), F32),
        pltpu.VMEM((256, 128), F32),
        pltpu.SemaphoreType.DMA((NT,)),
        pltpu.SemaphoreType.DMA((NT,)),
        pltpu.SemaphoreType.DMA((NT,)),
        pltpu.SemaphoreType.DMA((NT,)),
        pltpu.SemaphoreType.DMA((NT,)),
        pltpu.SemaphoreType.DMA((NT,)),
    ]
    if first:
        shapes.append(jax.ShapeDtypeStruct((1, 1), F32))
        outs.append(pl.BlockSpec(memory_space=pltpu.SMEM))
        scratch += [
            pltpu.VMEM((8, 128), F32),
            pltpu.VMEM((NC, 8, 128), F32),
            pltpu.SemaphoreType.DMA((NC,)),
            pltpu.SemaphoreType.DMA((NC,)),
        ]
    return pl.pallas_call(
        functools.partial(finish_body, first),
        out_shape=shapes,
        in_specs=[vmem] * 7,
        out_specs=outs,
        scratch_shapes=scratch,
        compiler_params=pltpu.CompilerParams(
            collective_id=1 if first else 3, has_side_effects=True, vmem_limit_bytes=30 * MIB
        ),
        name="finish" if first else "finish_more",
    )(grid, facts, over_r, over_x, over_t, lone_t, over_j)


def local(visibilities, kernels, destination, cell, plane):
    over_r, over_x = (jnp.asarray(t) for t in row_tables())
    over_t, over_j, lone_t = (jnp.asarray(t) for t in column_tables())
    samples = visibilities[0]
    dest = destination.reshape(1, BLK)
    kern = kernels.reshape(NW * 128, 128)
    recv, facts, table, weight = exchange(True, samples, dest, cell, plane, kern)
    grid = add_blocks(facts, recv, table, weight)
    image, most = finish(True, grid, facts, over_r, over_x, over_t, lone_t, over_j)
    most = most[0, 0]

    def more(image):
        def again(state):
            done, total = state
            skipped = jnp.broadcast_to(done, (1, BLK))
            recv, facts = exchange(False, samples, dest, cell, plane, skipped)
            grid = add_blocks(facts, recv, table, weight)
            [terms] = finish(False, grid, facts, over_r, over_x, over_t, lone_t, over_j)
            return done + CAP, total + terms

        return lax.while_loop(
            lambda state: state[0].astype(F32) < most, again, (jnp.int32(CAP), image)
        )[1]

    image = lax.cond(most > CAP, more, lambda terms: terms, image)
    return image.T


def solution(mesh):
    placed = (
        P("chan", "tile", None),
        P("chan", None, None, None, None),
        P("chan", "tile", None),
        P("chan", "tile"),
        P("chan", "tile"),
    )
    return jax.shard_map(
        local, mesh=mesh, in_specs=placed, out_specs=P("chan", "tile"), check_vma=False
    )
```
